512 devices in a mesh: row: 64 (over y, z), col: 8 (over x, core).
Axes of the slice: x: 4, y: 4, z: 16, core: 2. Of those that a mesh axis runs over, the one named last changes fastest.
Arguments:
- embeddings: bfloat16 [65536, 16384], P('row', 'col'), may hold values from -0.046875 to 0.046875
- targets: float32 [65536, 16], P('row'), may hold values from -64 to 64
- classes: int32 [65536], P('row'), may hold values 0 or 1
- start_coef: float32 [16384, 16], P('col'), may hold values from -6 to 6
Outputs:
- coef_next: float32 [16384, 16], P('col')
- resid_next: float32 [65536, 16], P('row')
- direction_next: float32 [16384, 16], P('col')
The draws below stay inside these ranges and needn't reach their ends.
All inputs are finite; a program needn't handle non-finite values. No bound on the sum of `classes` on one device may be relied on, other than what follows from the above.
Results may differ from the reference program's by a relative error of at most 0.0086.
Values sent between devices are 32-bit elements; how exact they have to be, the bound alone decides.
A program may use at most 64 MiB of HBM per device.

```python
import math
import jax
import jax.numpy as jnp
from jax import lax

D = 16384
K = 16
ROWS = 65536


def draw_targets(key, part):
    key = jax.random.fold_in(key, 7)
    key_base, key_scale = jax.random.split(key, 2)
    ramp = 1.0 + 7.0 * jnp.arange(ROWS, dtype=jnp.float32) / ROWS
    base = jax.random.normal(key_base, (ROWS, K), jnp.float32)
    row_scale = jnp.exp(jax.random.uniform(key_scale, (ROWS, 1), jnp.float32, math.log(0.5), math.log(2.0)))
    values = base * row_scale * ramp[:, None]
    return jnp.clip(values, -64.0, 64.0).astype(jnp.float32)


def plant(result, rng, least, top_value):
    dims = result.shape
    spot = [jax.random.randint(jax.random.fold_in(rng, axis), (), 0, dims[axis]) for axis in range(len(dims))]
    result = result.at[tuple(spot)].set(least)
    longest = dims.index(max(dims))
    spot[longest] = (spot[longest] + 1) % dims[longest]
    return result.at[tuple(spot)].set(top_value)


def levels(key, dims, shards, least, high):
    factor_of = 1.0
    for position, parts in shards:
        steps = jax.random.uniform(jax.random.fold_in(jax.random.fold_in(key, 6), position), (parts,), jnp.float32, least / len(shards), high / len(shards))
        factor_of = factor_of * jnp.repeat(jnp.exp(steps), dims[position] // parts).reshape((-1,) + (1,) * (len(dims) - 1 - position))
    return factor_of


def scatter_about(rng, extent, scale, bound, shards=(), kind=jnp.bfloat16):
    factor_of = levels(rng, extent, shards, -0.22, 0.18) if shards else 1.0
    values = jax.random.normal(rng, extent, jnp.float32) * scale * factor_of
    return jnp.minimum(jnp.maximum(values, -bound), bound).astype(kind)


def setup_inputs(seed: int = 0) -> dict:
    seeds = jax.random.split(jax.random.key(seed), 5)
    return {
        "embeddings": scatter_about(seeds[0], (ROWS, D), D ** -0.5, 0.046875, ((0, 64), (1, 8))),
        "targets": draw_targets(jax.random.fold_in(seeds[4], 71), 0),
        "classes": plant((jax.random.randint(seeds[2], (ROWS,), 0, 16) < 15).astype(jnp.int32), jax.random.fold_in(seeds[2], 1), 0, 1),
        "start_coef": scatter_about(seeds[3], (D, K), 1.0, 6.0, ((0, 8),), jnp.float32),
    }


huber_delta = 8.0

def transposed(left, right):
    return lax.dot_general(left, right, (((0,), (0,)), ((), ())), preferred_element_type=jnp.float32)

def reference(embeddings, targets, classes, start_coef):
    predicted = jnp.dot(embeddings, start_coef.astype(jnp.bfloat16), preferred_element_type=jnp.float32)
    resid_start = targets - predicted
    res_norm = jnp.sqrt(lax.optimization_barrier(jnp.sum(resid_start * resid_start, axis=1)))
    raw_weight = jnp.where(classes == 1, huber_delta / jnp.maximum(huber_delta, res_norm), jnp.float32(1.0))
    mean_weight = jnp.sum(raw_weight) / ROWS
    weighted = (raw_weight[:, None] * resid_start).astype(jnp.bfloat16)
    grad_raw = transposed(embeddings, weighted)
    gamma = lax.optimization_barrier(jnp.sum(grad_raw * grad_raw, axis=0)) / (mean_weight * mean_weight)
    image_raw = jnp.dot(embeddings, grad_raw.astype(jnp.bfloat16), preferred_element_type=jnp.float32)
    curvature = lax.optimization_barrier(jnp.sum(raw_weight[:, None] * image_raw * image_raw, axis=0)) / (mean_weight * mean_weight * mean_weight)
    alpha = gamma / curvature
    coef_next = start_coef + alpha * (grad_raw / mean_weight)
    resid_next = resid_start - alpha * (image_raw / mean_weight)
    weighted_next = (raw_weight[:, None] * resid_next).astype(jnp.bfloat16)
    grad_next = transposed(embeddings, weighted_next)
    beta = lax.optimization_barrier(jnp.sum(grad_next * grad_next, axis=0)) / (mean_weight * mean_weight) / gamma
    direction_next = grad_next / mean_weight + beta * (grad_raw / mean_weight)
    return (coef_next, resid_next, direction_next)
```

```python
import functools

import jax
import jax.numpy as jnp
from jax import lax
from jax.experimental import pallas as pl
from jax.experimental.pallas import tpu as pltpu
from jax.sharding import PartitionSpec as P

MESH = pl.DeviceIdType.MESH
huber_delta = 8.0
LANES = 128
PIECE = 4
Y_CHIPS = 4

BF16 = jnp.bfloat16
F32 = jnp.float32

(X1_RS, X1_AG, Y1_RS, Z1_RS, Z1_AG, Y1_AG, GAMMA, X2_RS, X2_AG,
 SCAL_Y, SCAL_Z, Y2_RS, Z2_RS, Z2_AG, Y2_AG, SQUARE) = range(16)


def drain(ref, sem):
    pltpu.make_async_copy(ref, ref, sem).wait()


def kernel(ny, nz, nc, resp, all_rows,
           e_hbm, t_hbm, cls_hbm, c_hbm,
           coef_out, resid_out, dir_out,
           e, t, cls, coef, cb, w, resid, lhs, g, gn,
           part, xrecv, xfull, yrecv, ypart, ysum, zrecv, gath,
           row_x, row_y, row_z, row_mine,
           load_sem, send_sem, recv_sem):
    rows_here, feats = e.shape
    quarter = feats // ny
    tiles = quarter // LANES
    per_tile = resp // PIECE
    here = lax.axis_index("row")
    col = lax.axis_index("col")
    y, z = lax.div(here, nz), lax.rem(here, nz)

    def x_peer(step):
        return here, lax.rem(col + step, nc)

    def y_peer(step):
        other = lax.rem(y + step, ny)
        return other * nz + z, col

    def z_peer(step):
        other = lax.rem(z + step, nz)
        return y * nz + other, col

    def far_first(k, n):
        return n // 2 + lax.div(k + 1, 2) * (2 * lax.rem(k, 2) - 1)

    def each(n, body):
        def step(k, _):
            body(far_first(k, n))
            return 0

        lax.fori_loop(0, n - 1, step, 0)

    def send(which, src, dst, peer):
        pltpu.make_async_remote_copy(
            src_ref=src, dst_ref=dst,
            send_sem=send_sem.at[which], recv_sem=recv_sem.at[which],
            device_id=peer, device_id_type=MESH,
        ).start()

    load_c = pltpu.make_async_copy(c_hbm, coef, load_sem.at[0])
    load_t = pltpu.make_async_copy(t_hbm, t, load_sem.at[1])
    load_cls = pltpu.make_async_copy(cls_hbm, cls, load_sem.at[2])
    load_c.start()

    def chunk(step):
        j = lax.rem(col + 1 + step, nc)
        rows = pl.ds(pl.multiple_of(j * LANES, LANES), LANES)
        return j, rows, pltpu.make_async_copy(
            e_hbm.at[rows], e.at[rows], load_sem.at[3 + step])

    for step in range(nc):
        chunk(step)[2].start()
    load_t.start()
    load_cls.start()

    barrier = pltpu.get_barrier_semaphore()

    def greet(peer_of):
        def inner(step):
            pl.semaphore_signal(barrier, inc=1, device_id=peer_of(step), device_id_type=MESH)
        return inner

    each(nc, greet(x_peer))
    each(ny, greet(y_peer))
    each(nz, greet(z_peer))

    def times_rows(left, rows):
        return lax.dot_general(
            left, e[rows, :], (((1,), (1,)), ((), ())), preferred_element_type=F32)

    def x_reduce(which_rs, which_ag, buf, after_first, loading, left):
        def product(step):
            j, rows, load = chunk(step)
            if loading:
                load.wait()
            part[buf, j] = times_rows(left[...], rows)
            return j

        first = product(0)
        after_first()
        send(which_rs, part.at[buf, first], xrecv.at[buf, col], (here, first))

        def more(step, _):
            j = product(step)
            send(which_rs, part.at[buf, j], xrecv.at[buf, col], (here, j))
            return 0

        lax.fori_loop(1, nc - 1, more, 0)
        product(nc - 1)
        xrecv[buf, col] = part[buf, col]
        drain(xrecv.at[buf, pl.ds(0, nc - 1)], recv_sem.at[which_rs])
        xfull[buf, col] = jnp.sum(xrecv[buf], axis=0)
        each(nc, lambda step: send(
            which_ag, xfull.at[buf, col], xfull.at[buf, col], x_peer(step)))
        drain(xfull.at[buf, pl.ds(0, nc - 1)], recv_sem.at[which_ag])

    def y_reduce(which, buf):
        def product(other):
            lanes = pl.ds(pl.multiple_of(other * quarter, quarter), quarter)
            both = jnp.dot(lhs[...], e[:, lanes], preferred_element_type=F32)
            total = both[:resp] + both[resp:]
            for tile in range(tiles):
                for q in range(per_tile):
                    ypart[buf, other, tile * per_tile + q] = total[
                        q * PIECE:(q + 1) * PIECE, tile * LANES:(tile + 1) * LANES]

        def more(k, _):
            other = lax.rem(y + far_first(k, ny), ny)
            product(other)
            send(which, ypart.at[buf, other], yrecv.at[buf, y], (other * nz + z, col))
            return 0

        lax.fori_loop(0, ny - 1, more, 0)
        product(y)
        yrecv[buf, y] = ypart[buf, y]

    def z_reduce(which_y, which_z, buf):
        drain(yrecv.at[buf, pl.ds(0, ny - 1)], recv_sem.at[which_y])
        ysum[buf] = jnp.sum(yrecv[buf], axis=0)
        each(nz, lambda step: send(
            which_z, ysum.at[buf, lax.rem(z + step, nz)], zrecv.at[buf, z], z_peer(step)))
        zrecv[buf, z] = ysum[buf, z]

    def z_gather(which_rs, which_ag, buf):
        drain(zrecv.at[buf, pl.ds(0, nz - 1)], recv_sem.at[which_rs])
        gath[buf, y, z] = jnp.sum(zrecv[buf], axis=0)
        each(nz, lambda step: send(
            which_ag, gath.at[buf, y, z], gath.at[buf, y, z], z_peer(step)))

    def y_gather(which_z, which_y, buf):
        drain(gath.at[buf, 0, pl.ds(0, nz - 1)], recv_sem.at[which_z])
        each(ny, lambda step: send(which_y, gath.at[buf, y], gath.at[buf, y], y_peer(step)))
        drain(gath.at[buf, pl.ds(0, ny - 1)], recv_sem.at[which_y])

    def assembled(buf, other, tile):
        return jnp.concatenate(
            [gath[buf, other, tile * per_tile + q] for q in range(per_tile)], axis=0)

    lane = lax.broadcasted_iota(jnp.int32, (resp, LANES), 1)
    sub = lax.broadcasted_iota(jnp.int32, (resp, LANES), 0)
    diagonal = lane == sub

    def to_row(column):
        return jnp.sum(jnp.where(diagonal, column, 0.0), axis=0, keepdims=True)

    def to_column(row):
        return jnp.sum(jnp.where(diagonal, row, 0.0), axis=1, keepdims=True)

    load_c.wait()
    cb[...] = coef[...].astype(BF16)
    x_reduce(X1_RS, X1_AG, 0,
             lambda: pl.semaphore_wait(barrier, (nc - 1) + (ny - 1) + (nz - 1)),
             True, cb)
    load_t.wait()
    load_cls.wait()

    def put_pair(j, value):
        high = value.astype(BF16)
        low = (value - high.astype(F32)).astype(BF16)
        lanes = slice(j * LANES, (j + 1) * LANES)
        lhs[0:resp, lanes] = high
        lhs[resp:2 * resp, lanes] = low

    for j in range(nc):
        r = t[:, j * LANES:(j + 1) * LANES] - xfull[0, j]
        resid[j] = r
        norm = jnp.sqrt(jnp.sum(r * r, axis=0, keepdims=True))
        weight = jnp.where(
            cls[j:j + 1, :] == 1, huber_delta / jnp.maximum(huber_delta, norm), 1.0)
        w[j:j + 1, :] = weight
        put_pair(j, weight * r)

    y_reduce(Y1_RS, 0)
    z_reduce(Y1_RS, Z1_RS, 0)
    z_gather(Z1_RS, Z1_AG, 0)
    y_gather(Z1_AG, Y1_AG, 0)
    norm2 = jnp.zeros((resp, LANES), F32)
    for other in range(ny):
        for tile in range(tiles):
            piece = assembled(0, other, tile)
            lanes = slice(other * quarter + tile * LANES, other * quarter + (tile + 1) * LANES)
            g[:, lanes] = piece
            cb[:, lanes] = piece.astype(BF16)
            norm2 = norm2 + piece * piece
    row_x[0, col] = to_row(jnp.sum(norm2, axis=1, keepdims=True))
    each(nc, lambda step: send(GAMMA, row_x.at[0, col], row_x.at[0, col], x_peer(step)))

    x_reduce(X2_RS, X2_AG, 1, lambda: None, False, cb)
    curv = jnp.zeros((resp, LANES), F32)
    weight_sum = jnp.zeros((1, LANES), F32)
    for j in range(nc):
        weight = w[j:j + 1, :]
        image = xfull[1, j]
        scaled = weight * image
        curv = curv + scaled * image
        weight_sum = weight_sum + weight
        put_pair(j, scaled)
    mine = to_row(jnp.sum(curv, axis=1, keepdims=True)) + jnp.where(
        lane[0:1] == resp, jnp.sum(weight_sum, axis=1, keepdims=True), 0.0)
    row_y[y] = mine
    each(ny, lambda step: send(SCAL_Y, row_y.at[y], row_y.at[y], y_peer(step)))

    y_reduce(Y2_RS, 1)
    drain(row_y.at[pl.ds(0, ny - 1)], recv_sem.at[SCAL_Y])
    row_z[z] = jnp.sum(row_y[...], axis=0)
    each(nz, lambda step: send(SCAL_Z, row_z.at[z], row_z.at[z], z_peer(step)))
    z_reduce(Y2_RS, Z2_RS, 1)

    drain(row_x.at[0, pl.ds(0, nc - 1)], recv_sem.at[GAMMA])
    drain(row_z.at[pl.ds(0, nz - 1)], recv_sem.at[SCAL_Z])
    sums = jnp.sum(row_z[...], axis=0)
    gamma_raw = to_column(jnp.sum(row_x[0], axis=0))
    curv_raw = to_column(sums)
    mean = jnp.sum(jnp.where(lane[0:1] == resp, sums, 0.0), axis=1, keepdims=True) / all_rows
    gamma = gamma_raw / (mean * mean)
    alpha = gamma / (curv_raw / (mean * mean * mean))
    z_gather(Z2_RS, Z2_AG, 1)
    coef_out[...] = coef[...] + alpha * (g[...] / mean)
    for j in range(nc):
        resid_out[:, j * LANES:(j + 1) * LANES] = resid[j] - alpha * (xfull[1, j] / mean)
    y_gather(Z2_AG, Y2_AG, 1)

    ratio = alpha / mean
    norm2 = jnp.zeros((resp, LANES), F32)
    for other in range(ny):
        for tile in range(tiles):
            lanes = slice(other * quarter + tile * LANES, other * quarter + (tile + 1) * LANES)
            piece = g[:, lanes] - ratio * assembled(1, other, tile)
            gn[:, lanes] = piece
            norm2 = norm2 + piece * piece
    row_x[1, col] = to_row(jnp.sum(norm2, axis=1, keepdims=True))
    each(nc, lambda step: send(SQUARE, row_x.at[1, col], row_x.at[1, col], x_peer(step)))
    drain(row_x.at[1, pl.ds(0, nc - 1)], recv_sem.at[SQUARE])
    square = to_column(jnp.sum(row_x[1], axis=0))
    beta = square / (mean * mean) / gamma
    dir_out[...] = gn[...] / mean + beta * (g[...] / mean)

    for which, ref in (
        (X1_RS, xrecv.at[0, pl.ds(0, nc - 1)]), (X2_RS, xrecv.at[1, pl.ds(0, nc - 1)]),
        (X1_AG, xfull.at[0, pl.ds(0, nc - 1)]), (X2_AG, xfull.at[1, pl.ds(0, nc - 1)]),
        (Y1_RS, yrecv.at[0, pl.ds(0, ny - 1)]), (Y2_RS, yrecv.at[1, pl.ds(0, ny - 1)]),
        (Z1_RS, zrecv.at[0, pl.ds(0, nz - 1)]), (Z2_RS, zrecv.at[1, pl.ds(0, nz - 1)]),
        (Z1_AG, zrecv.at[0, pl.ds(0, nz - 1)]), (Z2_AG, zrecv.at[1, pl.ds(0, nz - 1)]),
        (Y1_AG, gath.at[0, pl.ds(0, ny - 1)]), (Y2_AG, gath.at[1, pl.ds(0, ny - 1)]),
        (GAMMA, row_x.at[0, pl.ds(0, nc - 1)]), (SQUARE, row_x.at[1, pl.ds(0, nc - 1)]),
        (SCAL_Y, row_y.at[pl.ds(0, ny - 1)]), (SCAL_Z, row_z.at[pl.ds(0, nz - 1)]),
    ):
        drain(ref, send_sem.at[which])


def shards(ny, embeddings, targets, classes, start_coef):
    rows_here, feats = embeddings.shape
    resp = targets.shape[1]
    all_rows = rows_here * lax.axis_size("row")
    nc = lax.axis_size("col")
    nz = lax.axis_size("row") // ny
    vmem = pltpu.VMEM
    coef_next, resid_next, direction_next = pl.pallas_call(
        functools.partial(kernel, ny, nz, nc, resp, float(all_rows)),
        out_shape=(
            jax.ShapeDtypeStruct((resp, feats), F32),
            jax.ShapeDtypeStruct((resp, rows_here), F32),
            jax.ShapeDtypeStruct((resp, feats), F32),
        ),
        in_specs=[pl.BlockSpec(memory_space=pl.ANY)] * 4,
        out_specs=(pl.BlockSpec(memory_space=pltpu.VMEM),) * 3,
        scratch_shapes=[
            vmem((rows_here, feats), BF16),
            vmem((resp, rows_here), F32),
            vmem((nc, LANES), jnp.int32),
            vmem((resp, feats), F32),
            vmem((resp, feats), BF16),
            vmem((nc, LANES), F32),
            vmem((nc, resp, LANES), F32),
            vmem((2 * resp, rows_here), BF16),
            vmem((resp, feats), F32),
            vmem((resp, feats), F32),
            vmem((2, nc, resp, LANES), F32),
            vmem((2, nc, resp, LANES), F32),
            vmem((2, nc, resp, LANES), F32),
            vmem((2, ny, nz, PIECE, LANES), F32),
            vmem((2, ny, nz, PIECE, LANES), F32),
            vmem((2, nz, PIECE, LANES), F32),
            vmem((2, nz, PIECE, LANES), F32),
            vmem((2, ny, nz, PIECE, LANES), F32),
            vmem((2, nc, 1, LANES), F32),
            vmem((ny, 1, LANES), F32),
            vmem((nz, 1, LANES), F32),
            vmem((1, LANES), F32),
            pltpu.SemaphoreType.DMA((3 + nc,)),
            pltpu.SemaphoreType.DMA((16,)),
            pltpu.SemaphoreType.DMA((16,)),
        ],
        compiler_params=pltpu.CompilerParams(
            collective_id=0, has_side_effects=True, vmem_limit_bytes=32 * 1024 * 1024),
    )(embeddings, targets.T, classes.reshape(nc, LANES), start_coef.T)
    return coef_next.T, resid_next.T, direction_next.T


def solution(mesh, y_chips=Y_CHIPS):
    return jax.shard_map(
        functools.partial(shards, y_chips),
        mesh=mesh,
        in_specs=(P("row", "col"), P("row", None), P("row"), P("col", None)),
        out_specs=(P("col", None), P("row", None), P("col", None)),
        check_vma=False,
    )
```

```python
import functools

import jax
import jax.numpy as jnp
from jax import lax
from jax.experimental import pallas as pl
from jax.experimental.pallas import tpu as pltpu
from jax.sharding import PartitionSpec as P

MESH = pl.DeviceIdType.MESH
BF16 = jnp.bfloat16
F32 = jnp.float32
huber_delta = 8.0
LANES = 128
Y_CHIPS = 4
CORES = 2
CHUNKS = 4
LAG = 2

(X1, Y1, Z1, G1, GAMMA, X2, SCAL_Y, SCAL_Z, Y2, Z2, G2, SQUARE, CORE1) = range(13)
CORE2 = CORE1 + CHUNKS
N_SEMS = CORE2 + CHUNKS


def drain(ref, sem):
    pltpu.make_async_copy(ref, ref, sem).wait()


def kernel(ny, nz, nc, resp, all_rows,
           e_hbm, t_hbm, cls_hbm, c_hbm,
           coef_out, resid_out, dir_out,
           e, t, cls, coef, cb, w, resid, lhs, g, gn,
           part, whole, crecv, xsum, yrecv, ypart, ysum, zrecv, gath,
           row_x, row_y, row_z,
           load_sem, send_sem, recv_sem, near_sem):
    rows_here, feats = e.shape
    row_tiles = rows_here // LANES
    step_rows = rows_here // CHUNKS
    step_tiles = row_tiles // CHUNKS
    quarter = feats // ny
    pieces = quarter // LANES
    nx = nc // CORES
    near = nz // 8
    here = lax.axis_index("row")
    col = lax.axis_index("col")
    y, z = lax.div(here, nz), lax.rem(here, nz)
    x, core = lax.div(col, CORES), lax.rem(col, CORES)
    my_piece = lax.rem(z, pieces)

    def far_first(n):
        return [n // 2 + ((k + 1) // 2) * (2 * (k % 2) - 1) for k in range(n - 1)]

    def at_yz(dy, dz):
        return lax.rem(y + dy + ny, ny) * nz + lax.rem(z + dz + nz, nz), col

    def at_col(dc):
        return here, lax.rem(col + dc, nc)

    other_core = (here, col + 1 - 2 * core)
    x_mates = [(here, lax.rem(x + dx, nx) * CORES + core) for dx in far_first(nx)]
    col_mates = [at_col(dc) for dc in far_first(nc)]
    spread = [(dy, dz) for dz in sorted(range(1 - pieces // 2, pieces // 2 + 1), key=lambda d: -abs(d))
              for dy in [*far_first(ny), 0] if (dy, dz) != (0, 0)]

    def send(which, src, dst, peer):
        pltpu.make_async_remote_copy(
            src_ref=src, dst_ref=dst,
            send_sem=send_sem.at[which], recv_sem=recv_sem.at[which],
            device_id=peer, device_id_type=MESH,
        ).start()

    load_c = pltpu.make_async_copy(c_hbm, coef, load_sem.at[0])
    load_t = pltpu.make_async_copy(t_hbm, t, load_sem.at[1])
    load_cls = pltpu.make_async_copy(cls_hbm, cls, load_sem.at[2])
    load_e = [pltpu.make_async_copy(
        e_hbm.at[pl.ds(k * step_rows, step_rows)], e.at[pl.ds(k * step_rows, step_rows)],
        load_sem.at[3 + k]) for k in range(CHUNKS)]
    load_c.start()
    for load in load_e:
        load.start()
    load_t.start()
    load_cls.start()

    barrier = pltpu.get_barrier_semaphore()
    near_z = [dz for k in range(near) for dz in (near - k, k - near)]
    greeted = [*x_mates, *(at_yz(dy, 0) for dy in far_first(ny)), *(at_yz(0, dz) for dz in near_z), other_core]
    for peer in greeted:
        pl.semaphore_signal(barrier, inc=1, device_id=peer, device_id_type=MESH)

    def tell(k, reach):
        for i, dz in enumerate((reach, -reach)):
            pl.semaphore_signal(near_sem.at[2 * k + i], inc=1, device_id=at_yz(0, dz), device_id_type=MESH)

    def hear(k):
        for i in range(2):
            pl.semaphore_wait(near_sem.at[2 * k + i], 1)

    def meet():
        pl.semaphore_wait(barrier, len(greeted))
        tell(0, near)

    def x_reduce(which_core, which_x, buf, left, before_send):
        def product(k):
            if buf == 0:
                load_e[k].wait()
            both = lax.dot_general(
                left[...], e[k * step_rows:(k + 1) * step_rows, :], (((1,), (1,)), ((), ())),
                preferred_element_type=F32)
            for i in range(step_tiles):
                part[buf, k * step_tiles + i] = both[:, i * LANES:(i + 1) * LANES]
            if k == 0:
                before_send()
            tiles = pl.ds(k * step_tiles, step_tiles)
            send(which_core + k, part.at[buf, tiles], crecv.at[buf, tiles], other_core)

        def pass_on(k):
            tiles = pl.ds(k * step_tiles, step_tiles)
            drain(crecv.at[buf, tiles], recv_sem.at[which_core + k])
            xsum[buf, x, tiles] = part[buf, tiles] + crecv[buf, tiles]
            for mate in x_mates:
                send(which_x, xsum.at[buf, x, tiles], xsum.at[buf, x, tiles], mate)

        for k in range(CHUNKS + LAG):
            if k < CHUNKS:
                product(k)
            if k >= LAG:
                pass_on(k - LAG)
        drain(xsum.at[buf, pl.ds(0, nx - 1)], recv_sem.at[which_x])

    def x_total(buf, j):
        total = xsum[buf, 0, j]
        for k in range(1, nx):
            total = total + xsum[buf, k, j]
        return total

    def y_reduce(which, buf):
        for dy in [*far_first(ny), 0]:
            other = lax.rem(y + dy, ny)
            lanes = pl.ds(pl.multiple_of(other * quarter, quarter), quarter)
            both = jnp.dot(lhs[...], e[:, lanes], preferred_element_type=F32)
            total = both[:resp] + both[resp:]
            into = ypart.at[buf, other] if dy else yrecv.at[buf, y]
            for p in range(pieces):
                into[p] = total[:, p * LANES:(p + 1) * LANES]
            if dy:
                send(which, ypart.at[buf, other], yrecv.at[buf, y], at_yz(dy, 0))

    def z_reduce(which_y, which_z, buf):
        drain(yrecv.at[buf, pl.ds(0, ny - 1)], recv_sem.at[which_y])
        total = yrecv[buf, 0]
        for k in range(1, ny):
            total = total + yrecv[buf, k]
        ysum[buf] = total
        for dz in far_first(nz):
            peer_piece = lax.rem(z + dz, pieces)
            send(which_z, ysum.at[buf, peer_piece], zrecv.at[buf, z], at_yz(0, dz))
        zrecv[buf, z] = ysum[buf, my_piece]

    def spread_out(which_z, which_g, buf):
        drain(zrecv.at[buf, pl.ds(0, nz - 1)], recv_sem.at[which_z])
        total = zrecv[buf, 0]
        for k in range(1, nz):
            total = total + zrecv[buf, k]
        gath[buf, y, my_piece] = total
        for dy, dz in spread:
            send(which_g, gath.at[buf, y, my_piece], gath.at[buf, y, my_piece], at_yz(dy, dz))

    def collect(which_g, buf):
        drain(zrecv.at[buf, pl.ds(0, ny * pieces - 1)], recv_sem.at[which_g])

    lane = lax.broadcasted_iota(jnp.int32, (resp, LANES), 1)
    sub = lax.broadcasted_iota(jnp.int32, (resp, LANES), 0)
    diagonal = lane == sub

    def to_row(column):
        return jnp.sum(jnp.where(diagonal, column, 0.0), axis=0, keepdims=True)

    def to_column(row):
        return jnp.sum(jnp.where(diagonal, row, 0.0), axis=1, keepdims=True)

    load_c.wait()
    cb[...] = coef[...].astype(BF16)
    x_reduce(CORE1, X1, 0, cb, meet)
    load_t.wait()
    load_cls.wait()
    hear(0)
    tell(1, 2 * near)

    def put_pair(j, value):
        high = value.astype(BF16)
        low = (value - high.astype(F32)).astype(BF16)
        lanes = slice(j * LANES, (j + 1) * LANES)
        lhs[0:resp, lanes] = high
        lhs[resp:2 * resp, lanes] = low

    for j in range(row_tiles):
        r = t[:, j * LANES:(j + 1) * LANES] - x_total(0, j)
        resid[j] = r
        norm = jnp.sqrt(jnp.sum(r * r, axis=0, keepdims=True))
        weight = jnp.where(
            cls[j:j + 1, :] == 1, huber_delta / jnp.maximum(huber_delta, norm), 1.0)
        w[j:j + 1, :] = weight
        put_pair(j, weight * r)

    y_reduce(Y1, 0)
    hear(1)
    z_reduce(Y1, Z1, 0)
    spread_out(Z1, G1, 0)
    collect(G1, 0)
    norm2 = jnp.zeros((resp, LANES), F32)
    for other in range(ny):
        for p in range(pieces):
            piece = gath[0, other, p]
            lanes = slice(other * quarter + p * LANES, other * quarter + (p + 1) * LANES)
            g[:, lanes] = piece
            cb[:, lanes] = piece.astype(BF16)
            norm2 = norm2 + piece * piece
    row_x[0, col] = to_row(jnp.sum(norm2, axis=1, keepdims=True))
    for mate in col_mates:
        send(GAMMA, row_x.at[0, col], row_x.at[0, col], mate)

    x_reduce(CORE2, X2, 1, cb, lambda: None)
    curv = jnp.zeros((resp, LANES), F32)
    weight_sum = jnp.zeros((1, LANES), F32)
    for j in range(row_tiles):
        weight = w[j:j + 1, :]
        image = x_total(1, j)
        whole[j] = image
        scaled = weight * image
        curv = curv + scaled * image
        weight_sum = weight_sum + weight
        put_pair(j, scaled)
    row_y[y] = to_row(jnp.sum(curv, axis=1, keepdims=True)) + jnp.where(
        lane[0:1] == resp, jnp.sum(weight_sum, axis=1, keepdims=True), 0.0)
    for dy in far_first(ny):
        send(SCAL_Y, row_y.at[y], row_y.at[y], at_yz(dy, 0))

    y_reduce(Y2, 1)
    drain(row_y.at[pl.ds(0, ny - 1)], recv_sem.at[SCAL_Y])
    row_z[z] = jnp.sum(row_y[...], axis=0)
    for dz in far_first(nz):
        send(SCAL_Z, row_z.at[z], row_z.at[z], at_yz(0, dz))
    z_reduce(Y2, Z2, 1)

    drain(row_x.at[0, pl.ds(0, nc - 1)], recv_sem.at[GAMMA])
    drain(row_z.at[pl.ds(0, nz - 1)], recv_sem.at[SCAL_Z])
    sums = jnp.sum(row_z[...], axis=0)
    gamma_raw = to_column(jnp.sum(row_x[0], axis=0))
    curv_raw = to_column(sums)
    mean = jnp.sum(jnp.where(lane[0:1] == resp, sums, 0.0), axis=1, keepdims=True) / all_rows
    gamma = gamma_raw / (mean * mean)
    alpha = gamma / (curv_raw / (mean * mean * mean))
    ratio = alpha / mean
    coef_out[...] = coef[...] + alpha * (g[...] / mean)
    for j in range(row_tiles):
        resid_out[:, j * LANES:(j + 1) * LANES] = resid[j] - alpha * (whole[j] / mean)
    spread_out(Z2, G2, 1)
    collect(G2, 1)

    norm2 = jnp.zeros((resp, LANES), F32)
    for other in range(ny):
        for p in range(pieces):
            lanes = slice(other * quarter + p * LANES, other * quarter + (p + 1) * LANES)
            piece = g[:, lanes] - ratio * gath[1, other, p]
            gn[:, lanes] = piece
            norm2 = norm2 + piece * piece
    row_x[1, col] = to_row(jnp.sum(norm2, axis=1, keepdims=True))
    for mate in col_mates:
        send(SQUARE, row_x.at[1, col], row_x.at[1, col], mate)
    drain(row_x.at[1, pl.ds(0, nc - 1)], recv_sem.at[SQUARE])
    square = to_column(jnp.sum(row_x[1], axis=0))
    beta = square / (mean * mean) / gamma
    dir_out[...] = gn[...] / mean + beta * (g[...] / mean)

    for which, ref in (
        (X1, xsum.at[0, pl.ds(0, nx - 1)]), (X2, xsum.at[1, pl.ds(0, nx - 1)]),
        (Y1, yrecv.at[0, pl.ds(0, ny - 1)]), (Y2, yrecv.at[1, pl.ds(0, ny - 1)]),
        (Z1, zrecv.at[0, pl.ds(0, nz - 1)]), (Z2, zrecv.at[1, pl.ds(0, nz - 1)]),
        (G1, zrecv.at[0, pl.ds(0, ny * pieces - 1)]), (G2, zrecv.at[1, pl.ds(0, ny * pieces - 1)]),
        (GAMMA, row_x.at[0, pl.ds(0, nc - 1)]), (SQUARE, row_x.at[1, pl.ds(0, nc - 1)]),
        (SCAL_Y, row_y.at[pl.ds(0, ny - 1)]), (SCAL_Z, row_z.at[pl.ds(0, nz - 1)]),
        *((base + k, crecv.at[0, pl.ds(0, step_tiles)]) for base in (CORE1, CORE2) for k in range(CHUNKS)),
    ):
        drain(ref, send_sem.at[which])


def write_out(a_in, b_in, c_in, a_out, b_out, c_out, sems):
    copies = [pltpu.make_async_copy(src, dst, sems.at[k])
              for k, (src, dst) in enumerate(((a_in, a_out), (b_in, b_out), (c_in, c_out)))]
    for copy in copies:
        copy.start()
    for copy in copies:
        copy.wait()


def shards(ny, embeddings, targets, classes, start_coef):
    rows_here, feats = embeddings.shape
    resp = targets.shape[1]
    all_rows = rows_here * lax.axis_size("row")
    nc = lax.axis_size("col")
    nz = lax.axis_size("row") // ny
    row_tiles = rows_here // LANES
    pieces = feats // ny // LANES
    vmem = pltpu.VMEM
    outs = (
        jax.ShapeDtypeStruct((resp, feats), F32),
        jax.ShapeDtypeStruct((resp, rows_here), F32),
        jax.ShapeDtypeStruct((resp, feats), F32),
    )
    results = pl.pallas_call(
        functools.partial(kernel, ny, nz, nc, resp, float(all_rows)),
        out_shape=outs,
        in_specs=[pl.BlockSpec(memory_space=pl.ANY)] * 4,
        out_specs=(pl.BlockSpec(memory_space=pltpu.VMEM),) * 3,
        scratch_shapes=[
            vmem((rows_here, feats), BF16),
            vmem((resp, rows_here), F32),
            vmem((row_tiles, LANES), jnp.int32),
            vmem((resp, feats), F32),
            vmem((resp, feats), BF16),
            vmem((row_tiles, LANES), F32),
            vmem((row_tiles, resp, LANES), F32),
            vmem((2 * resp, rows_here), BF16),
            vmem((resp, feats), F32),
            vmem((resp, feats), F32),
            vmem((2, row_tiles, resp, LANES), F32),
            vmem((row_tiles, resp, LANES), F32),
            vmem((2, row_tiles, resp, LANES), F32),
            vmem((2, nc // CORES, row_tiles, resp, LANES), F32),
            vmem((2, ny, pieces, resp, LANES), F32),
            vmem((2, ny, pieces, resp, LANES), F32),
            vmem((2, pieces, resp, LANES), F32),
            vmem((2, max(nz, ny * pieces), resp, LANES), F32),
            vmem((2, ny, pieces, resp, LANES), F32),
            vmem((2, nc, 1, LANES), F32),
            vmem((ny, 1, LANES), F32),
            vmem((nz, 1, LANES), F32),
            pltpu.SemaphoreType.DMA((3 + CHUNKS,)),
            pltpu.SemaphoreType.DMA((N_SEMS,)),
            pltpu.SemaphoreType.DMA((N_SEMS,)),
            pltpu.SemaphoreType.REGULAR((4,)),
        ],
        compiler_params=pltpu.CompilerParams(
            collective_id=0, has_side_effects=True, vmem_limit_bytes=60 * 1024 * 1024),
    )(embeddings, targets.T, classes.reshape(row_tiles, LANES), start_coef.T)
    results = pl.pallas_call(
        write_out,
        out_shape=outs,
        in_specs=[pl.BlockSpec(memory_space=pl.ANY)] * 3,
        out_specs=(pl.BlockSpec(memory_space=pl.ANY),) * 3,
        scratch_shapes=[pltpu.SemaphoreType.DMA((3,))],
    )(*results)
    return tuple(out.T for out in results)


def solution(mesh, y_chips=Y_CHIPS):
    return jax.shard_map(
        functools.partial(shards, y_chips),
        mesh=mesh,
        in_specs=(P("row", "col"), P("row", None), P("row"), P("col", None)),
        out_specs=(P("col", None), P("row", None), P("col", None)),
        check_vma=False,
    )
```

```python
import functools

import jax
import jax.numpy as jnp
from jax import lax
from jax.experimental import pallas as pl
from jax.experimental.pallas import tpu as pltpu
from jax.sharding import PartitionSpec as P

MESH = pl.DeviceIdType.MESH
BF16 = jnp.bfloat16
F32 = jnp.float32
huber_delta = 8.0
LANES = 128
Y_CHIPS = 4
CORES = 2
CHUNKS = 2

(Y1, Z1, GAMMA, SCAL_Y, SCAL_Z, Y2, Z2, SQUARE, CORE1) = range(9)
CORE2 = CORE1 + CHUNKS
X1 = CORE2 + CHUNKS
X2 = X1 + CHUNKS
G1 = X2 + CHUNKS
G2 = G1 + Y_CHIPS
N_SEMS = G2 + Y_CHIPS


def drain(ref, sem):
    pltpu.make_async_copy(ref, ref, sem).wait()


def kernel(ny, nz, nc, resp, all_rows,
           e_hbm, t_hbm, cls_hbm, c_hbm,
           coef_out, resid_out, dir_out,
           e, t, cls, coef, cb, acc, gacc, w, resid, lhs, g, gn,
           part, whole, crecv, xsum, yrecv, ypart, ysum, zrecv, gath,
           row_x, row_y, row_z,
           load_sem, send_sem, recv_sem, near_sem):
    rows_here, feats = e.shape
    row_tiles = rows_here // LANES
    step_rows = rows_here // CHUNKS
    step_tiles = row_tiles // CHUNKS
    quarter = feats // ny
    pieces = quarter // LANES
    nx = nc // CORES
    near = nz // 8
    here = lax.axis_index("row")
    col = lax.axis_index("col")
    y, z = lax.div(here, nz), lax.rem(here, nz)
    x, core = lax.div(col, CORES), lax.rem(col, CORES)
    my_piece = lax.rem(z, pieces)

    def far_first(n):
        return [n // 2 + ((k + 1) // 2) * (2 * (k % 2) - 1) for k in range(n - 1)]

    def at_yz(dy, dz):
        return lax.rem(y + dy + ny, ny) * nz + lax.rem(z + dz + nz, nz), col

    def at_col(dc):
        return here, lax.rem(col + dc, nc)

    other_core = (here, col + 1 - 2 * core)
    x_mates = [(here, lax.rem(x + dx, nx) * CORES + core) for dx in far_first(nx)]
    col_mates = [at_col(dc) for dc in far_first(nc)]
    spread = [(dy, dz) for dz in sorted(range(1 - pieces // 2, pieces // 2 + 1), key=lambda d: -abs(d))
              for dy in [*far_first(ny), 0] if (dy, dz) != (0, 0)]

    def send(which, src, dst, peer):
        pltpu.make_async_remote_copy(
            src_ref=src, dst_ref=dst,
            send_sem=send_sem.at[which], recv_sem=recv_sem.at[which],
            device_id=peer, device_id_type=MESH,
        ).start()

    load_c = pltpu.make_async_copy(c_hbm, coef, load_sem.at[0])
    load_t = pltpu.make_async_copy(t_hbm, t, load_sem.at[1])
    load_cls = pltpu.make_async_copy(cls_hbm, cls, load_sem.at[2])
    load_e = [pltpu.make_async_copy(
        e_hbm.at[pl.ds(k * step_rows, step_rows)], e.at[pl.ds(k * step_rows, step_rows)],
        load_sem.at[3 + k]) for k in range(CHUNKS)]
    load_c.start()
    for load in load_e:
        load.start()
    load_t.start()
    load_cls.start()

    barrier = pltpu.get_barrier_semaphore()
    near_z = [dz for k in range(near) for dz in (near - k, k - near)]
    greeted = [*x_mates, *(at_yz(dy, 0) for dy in far_first(ny)), *(at_yz(0, dz) for dz in near_z), other_core]
    for peer in greeted:
        pl.semaphore_signal(barrier, inc=1, device_id=peer, device_id_type=MESH)

    def tell(k, reach):
        for i, dz in enumerate((reach, -reach)):
            pl.semaphore_signal(near_sem.at[2 * k + i], inc=1, device_id=at_yz(0, dz), device_id_type=MESH)

    def hear(k):
        for i in range(2):
            pl.semaphore_wait(near_sem.at[2 * k + i], 1)

    def meet():
        pl.semaphore_wait(barrier, len(greeted))
        tell(0, near)

    def x_send(which_core, which_x, buf, product, before_send, between):
        for k in range(CHUNKS):
            both = product(slice(k * step_rows, (k + 1) * step_rows), k)
            for i in range(step_tiles):
                part[buf, k * step_tiles + i] = both[:, i * LANES:(i + 1) * LANES]
            if k == 0:
                before_send()
            tiles = pl.ds(k * step_tiles, step_tiles)
            send(which_core + k, part.at[buf, tiles], crecv.at[buf, tiles], other_core)
        between()
        for k in range(CHUNKS):
            tiles = pl.ds(k * step_tiles, step_tiles)
            drain(crecv.at[buf, tiles], recv_sem.at[which_core + k])
            xsum[buf, x, tiles] = part[buf, tiles] + crecv[buf, tiles]
            for mate in x_mates:
                send(which_x + k, xsum.at[buf, x, tiles], xsum.at[buf, x, tiles], mate)

    def against_rows(left, rows, lanes):
        return lax.dot_general(
            left, e[rows, lanes], (((1,), (1,)), ((), ())), preferred_element_type=F32)

    def x_chunks(which_x, buf, of_tile):
        for k in range(CHUNKS):
            drain(xsum.at[buf, pl.ds(0, nx - 1), pl.ds(0, step_tiles)], recv_sem.at[which_x + k])
            for j in range(k * step_tiles, (k + 1) * step_tiles):
                of_tile(j)
            if k < CHUNKS - 1:
                rows = slice(k * step_rows, (k + 1) * step_rows)
                both = jnp.dot(lhs[:, rows], e[rows, :], preferred_element_type=F32)
                total = both[:resp] + both[resp:]
                gacc[...] = total if k == 0 else gacc[...] + total

    def x_total(buf, j):
        total = xsum[buf, 0, j]
        for k in range(1, nx):
            total = total + xsum[buf, k, j]
        return total

    def y_reduce(which, buf):
        for dy in [*far_first(ny), 0]:
            other = lax.rem(y + dy, ny)
            lanes = pl.ds(pl.multiple_of(other * quarter, quarter), quarter)
            rows = slice((CHUNKS - 1) * step_rows, CHUNKS * step_rows)
            both = jnp.dot(lhs[:, rows], e[rows, lanes], preferred_element_type=F32)
            total = gacc[:, lanes] + both[:resp] + both[resp:]
            into = ypart.at[buf, other] if dy else yrecv.at[buf, y]
            for p in range(pieces):
                into[p] = total[:, p * LANES:(p + 1) * LANES]
            if dy:
                send(which, ypart.at[buf, other], yrecv.at[buf, y], at_yz(dy, 0))

    def z_reduce(which_y, which_z, buf):
        drain(yrecv.at[buf, pl.ds(0, ny - 1)], recv_sem.at[which_y])
        total = yrecv[buf, 0]
        for k in range(1, ny):
            total = total + yrecv[buf, k]
        ysum[buf] = total
        for dz in far_first(nz):
            peer_piece = lax.rem(z + dz, pieces)
            send(which_z, ysum.at[buf, peer_piece], zrecv.at[buf, z], at_yz(0, dz))
        zrecv[buf, z] = ysum[buf, my_piece]

    def spread_out(which_z, which_g, buf):
        drain(zrecv.at[buf, pl.ds(0, nz - 1)], recv_sem.at[which_z])
        total = zrecv[buf, 0]
        for k in range(1, nz):
            total = total + zrecv[buf, k]
        gath[buf, y, my_piece] = total
        for dy, dz in spread:
            send(which_g + dy, gath.at[buf, y, my_piece], gath.at[buf, y, my_piece], at_yz(dy, dz))

    def collect(which_g, buf, dy):
        drain(zrecv.at[buf, pl.ds(0, pieces if dy else pieces - 1)], recv_sem.at[which_g + dy])
        return lax.rem(y - dy + ny, ny)

    by_arrival = [0, *reversed(far_first(ny))]

    lane = lax.broadcasted_iota(jnp.int32, (resp, LANES), 1)
    sub = lax.broadcasted_iota(jnp.int32, (resp, LANES), 0)
    diagonal = lane == sub

    def to_row(column):
        return jnp.sum(jnp.where(diagonal, column, 0.0), axis=0, keepdims=True)

    def to_column(row):
        return jnp.sum(jnp.where(diagonal, row, 0.0), axis=1, keepdims=True)

    load_c.wait()
    cb[...] = coef[...].astype(BF16)

    def first_product(rows, k):
        load_e[k].wait()
        return against_rows(cb[...], rows, slice(None))

    x_send(CORE1, X1, 0, first_product, meet, lambda: None)
    load_t.wait()
    load_cls.wait()
    hear(0)
    tell(1, 2 * near)

    def put_pair(j, value):
        high = value.astype(BF16)
        low = (value - high.astype(F32)).astype(BF16)
        lanes = slice(j * LANES, (j + 1) * LANES)
        lhs[0:resp, lanes] = high
        lhs[resp:2 * resp, lanes] = low

    def weigh(j):
        r = t[:, j * LANES:(j + 1) * LANES] - x_total(0, j)
        resid[j] = r
        norm = jnp.sqrt(jnp.sum(r * r, axis=0, keepdims=True))
        weight = jnp.where(
            cls[j:j + 1, :] == 1, huber_delta / jnp.maximum(huber_delta, norm), 1.0)
        w[j:j + 1, :] = weight
        put_pair(j, weight * r)

    x_chunks(X1, 0, weigh)

    y_reduce(Y1, 0)
    hear(1)
    z_reduce(Y1, Z1, 0)
    spread_out(Z1, G1, 0)
    for k, dy in enumerate(by_arrival):
        behind = collect(G1, 0, dy)
        for p in range(pieces):
            lanes = pl.ds(pl.multiple_of(behind * quarter + p * LANES, LANES), LANES)
            piece = gath[0, behind, p]
            g[:, lanes] = piece
            cb[:, lanes] = piece.astype(BF16)
        lanes = pl.ds(pl.multiple_of(behind * quarter, quarter), quarter)
        if k < ny - 1:
            share = against_rows(cb[:, lanes], slice(None), lanes)
            acc[...] = share if k == 0 else acc[...] + share

    def last_product(rows, k):
        return acc[:, rows] + against_rows(cb[:, lanes], rows, lanes)

    def send_gamma():
        norm2 = jnp.zeros((resp, LANES), F32)
        for p in range(ny * pieces):
            piece = g[:, p * LANES:(p + 1) * LANES]
            norm2 = norm2 + piece * piece
        row_x[0, col] = to_row(jnp.sum(norm2, axis=1, keepdims=True))
        for mate in col_mates:
            send(GAMMA, row_x.at[0, col], row_x.at[0, col], mate)

    x_send(CORE2, X2, 1, last_product, lambda: None, send_gamma)
    sums = [jnp.zeros((resp, LANES), F32), jnp.zeros((1, LANES), F32)]

    def weigh_image(j):
        weight = w[j:j + 1, :]
        image = x_total(1, j)
        whole[j] = image
        scaled = weight * image
        sums[0] = sums[0] + scaled * image
        sums[1] = sums[1] + weight
        put_pair(j, scaled)

    x_chunks(X2, 1, weigh_image)
    curv, weight_sum = sums
    row_y[y] = to_row(jnp.sum(curv, axis=1, keepdims=True)) + jnp.where(
        lane[0:1] == resp, jnp.sum(weight_sum, axis=1, keepdims=True), 0.0)
    for dy in far_first(ny):
        send(SCAL_Y, row_y.at[y], row_y.at[y], at_yz(dy, 0))

    y_reduce(Y2, 1)
    drain(row_y.at[pl.ds(0, ny - 1)], recv_sem.at[SCAL_Y])
    row_z[z] = jnp.sum(row_y[...], axis=0)
    for dz in far_first(nz):
        send(SCAL_Z, row_z.at[z], row_z.at[z], at_yz(0, dz))
    z_reduce(Y2, Z2, 1)

    drain(row_x.at[0, pl.ds(0, nc - 1)], recv_sem.at[GAMMA])
    drain(row_z.at[pl.ds(0, nz - 1)], recv_sem.at[SCAL_Z])
    sums = jnp.sum(row_z[...], axis=0)
    gamma_raw = to_column(jnp.sum(row_x[0], axis=0))
    curv_raw = to_column(sums)
    mean = jnp.sum(jnp.where(lane[0:1] == resp, sums, 0.0), axis=1, keepdims=True) / all_rows
    gamma = gamma_raw / (mean * mean)
    alpha = gamma / (curv_raw / (mean * mean * mean))
    ratio = alpha / mean
    coef_out[...] = coef[...] + alpha * (g[...] / mean)
    for j in range(row_tiles):
        resid_out[:, j * LANES:(j + 1) * LANES] = resid[j] - alpha * (whole[j] / mean)
    spread_out(Z2, G2, 1)
    for dy in by_arrival:
        collect(G2, 1, dy)

    norm2 = jnp.zeros((resp, LANES), F32)
    for other in range(ny):
        for p in range(pieces):
            lanes = slice(other * quarter + p * LANES, other * quarter + (p + 1) * LANES)
            piece = g[:, lanes] - ratio * gath[1, other, p]
            gn[:, lanes] = piece
            norm2 = norm2 + piece * piece
    row_x[1, col] = to_row(jnp.sum(norm2, axis=1, keepdims=True))
    for mate in col_mates:
        send(SQUARE, row_x.at[1, col], row_x.at[1, col], mate)
    drain(row_x.at[1, pl.ds(0, nc - 1)], recv_sem.at[SQUARE])
    square = to_column(jnp.sum(row_x[1], axis=0))
    beta = square / (mean * mean) / gamma
    dir_out[...] = gn[...] / mean + beta * (g[...] / mean)

    for which, ref in (
        (Y1, yrecv.at[0, pl.ds(0, ny - 1)]), (Y2, yrecv.at[1, pl.ds(0, ny - 1)]),
        (Z1, zrecv.at[0, pl.ds(0, nz - 1)]), (Z2, zrecv.at[1, pl.ds(0, nz - 1)]),
        (GAMMA, row_x.at[0, pl.ds(0, nc - 1)]), (SQUARE, row_x.at[1, pl.ds(0, nc - 1)]),
        (SCAL_Y, row_y.at[pl.ds(0, ny - 1)]), (SCAL_Z, row_z.at[pl.ds(0, nz - 1)]),
        *((base + k, crecv.at[0, pl.ds(0, step_tiles)]) for base in (CORE1, CORE2) for k in range(CHUNKS)),
        *((base + k, xsum.at[0, pl.ds(0, nx - 1), pl.ds(0, step_tiles)]) for base in (X1, X2) for k in range(CHUNKS)),
        *((base + k, zrecv.at[0, pl.ds(0, pieces if k else pieces - 1)]) for base in (G1, G2) for k in range(ny)),
    ):
        drain(ref, send_sem.at[which])


def write_out(a_in, b_in, c_in, a_out, b_out, c_out, sems):
    copies = [pltpu.make_async_copy(src, dst, sems.at[k])
              for k, (src, dst) in enumerate(((a_in, a_out), (b_in, b_out), (c_in, c_out)))]
    for copy in copies:
        copy.start()
    for copy in copies:
        copy.wait()


def shards(ny, embeddings, targets, classes, start_coef):
    rows_here, feats = embeddings.shape
    resp = targets.shape[1]
    all_rows = rows_here * lax.axis_size("row")
    nc = lax.axis_size("col")
    nz = lax.axis_size("row") // ny
    row_tiles = rows_here // LANES
    pieces = feats // ny // LANES
    vmem = pltpu.VMEM
    outs = (
        jax.ShapeDtypeStruct((resp, feats), F32),
        jax.ShapeDtypeStruct((resp, rows_here), F32),
        jax.ShapeDtypeStruct((resp, feats), F32),
    )
    results = pl.pallas_call(
        functools.partial(kernel, ny, nz, nc, resp, float(all_rows)),
        out_shape=outs,
        in_specs=[pl.BlockSpec(memory_space=pltpu.HBM)] * 4,
        out_specs=(pl.BlockSpec(memory_space=pltpu.VMEM),) * 3,
        scratch_shapes=[
            vmem((rows_here, feats), BF16),
            vmem((resp, rows_here), F32),
            vmem((row_tiles, LANES), jnp.int32),
            vmem((resp, feats), F32),
            vmem((resp, feats), BF16),
            vmem((resp, rows_here), F32),
            vmem((resp, feats), F32),
            vmem((row_tiles, LANES), F32),
            vmem((row_tiles, resp, LANES), F32),
            vmem((2 * resp, rows_here), BF16),
            vmem((resp, feats), F32),
            vmem((resp, feats), F32),
            vmem((2, row_tiles, resp, LANES), F32),
            vmem((row_tiles, resp, LANES), F32),
            vmem((2, row_tiles, resp, LANES), F32),
            vmem((2, nc // CORES, row_tiles, resp, LANES), F32),
            vmem((2, ny, pieces, resp, LANES), F32),
            vmem((2, ny, pieces, resp, LANES), F32),
            vmem((2, pieces, resp, LANES), F32),
            vmem((2, max(nz, ny * pieces), resp, LANES), F32),
            vmem((2, ny, pieces, resp, LANES), F32),
            vmem((2, nc, 1, LANES), F32),
            vmem((ny, 1, LANES), F32),
            vmem((nz, 1, LANES), F32),
            pltpu.SemaphoreType.DMA((3 + CHUNKS,)),
            pltpu.SemaphoreType.DMA((N_SEMS,)),
            pltpu.SemaphoreType.DMA((N_SEMS,)),
            pltpu.SemaphoreType.REGULAR((4,)),
        ],
        compiler_params=pltpu.CompilerParams(
            collective_id=0, has_side_effects=True, vmem_limit_bytes=60 * 1024 * 1024),
    )(embeddings, targets.T, classes.reshape(row_tiles, LANES), start_coef.T)
    results = pl.pallas_call(
        write_out,
        out_shape=outs,
        in_specs=[pl.BlockSpec(memory_space=pltpu.VMEM)] * 3,
        out_specs=(pl.BlockSpec(memory_space=pl.ANY),) * 3,
        scratch_shapes=[pltpu.SemaphoreType.DMA((3,))],
        compiler_params=pltpu.CompilerParams(vmem_limit_bytes=60 * 1024 * 1024),
    )(*results)
    return tuple(out.T for out in results)


def solution(mesh, y_chips=Y_CHIPS):
    return jax.shard_map(
        functools.partial(shards, y_chips),
        mesh=mesh,
        in_specs=(P("row", "col"), P("row", None), P("row"), P("col", None)),
        out_specs=(P("col", None), P("row", None), P("col", None)),
        check_vma=False,
    )
```

```python
import functools

import jax
import jax.numpy as jnp
from jax import lax
from jax.experimental import pallas as pl
from jax.experimental.pallas import tpu as pltpu
from jax.sharding import PartitionSpec as P

MESH = pl.DeviceIdType.MESH
BF16 = jnp.bfloat16
F32 = jnp.float32
huber_delta = 8.0
LANES = 128
Y_CHIPS = 4
CORES = 2

(CORE1, X1, BACK1, Y1, Z1, GAMMA, CORE2, X2, BACK2, SCAL_Y, SCAL_Z, Y2, Z2, SQUARE, G1) = range(15)
G2 = G1 + Y_CHIPS
N_SEMS = G2 + Y_CHIPS


def drain(ref, sem):
    pltpu.make_async_copy(ref, ref, sem).wait()


def kernel(ny, nz, nc, resp, all_rows,
           e_hbm, t_hbm, cls_hbm, c_hbm,
           coef_out, resid_out, dir_out,
           e, t, cls, coef, cb, acc, gacc, w, resid, lhs, g,
           part, crecv, xsum, xfull, yrecv, ypart, ysum, zrecv, gath,
           row_x, row_y, row_z, row_sq,
           load_sem, send_sem, recv_sem, near_sem):
    rows_here, feats = e.shape
    row_tiles = rows_here // LANES
    half_rows = rows_here // CORES
    half_tiles = row_tiles // CORES
    quarter = feats // ny
    pieces = quarter // LANES
    nx = nc // CORES
    near = nz // 8
    here = lax.axis_index("row")
    col = lax.axis_index("col")
    y, z = lax.div(here, nz), lax.rem(here, nz)
    x, core = lax.div(col, CORES), lax.rem(col, CORES)
    my_piece = lax.rem(z, pieces)
    theirs = 1 - core

    def tile_at(j):
        return pl.ds(pl.multiple_of(j * LANES, LANES), LANES)

    def rows_of(k):
        return pl.ds(pl.multiple_of(k * half_rows, half_rows), half_rows)

    def tiles_of(k):
        return pl.ds(k * half_tiles, half_tiles)

    def far_first(n):
        return [n // 2 + ((k + 1) // 2) * (2 * (k % 2) - 1) for k in range(n - 1)]

    def at_yz(dy, dz):
        return lax.rem(y + dy + ny, ny) * nz + lax.rem(z + dz + nz, nz), col

    def at_col(dc):
        return here, lax.rem(col + dc, nc)

    other_core = (here, col + 1 - 2 * core)
    x_mates = [(here, lax.rem(x + dx, nx) * CORES + core) for dx in far_first(nx)]
    col_mates = [at_col(dc) for dc in far_first(nc)]
    spread = [(dy, dz) for dz in sorted(range(1 - pieces // 2, pieces // 2 + 1), key=lambda d: -abs(d))
              for dy in [*far_first(ny), 0] if (dy, dz) != (0, 0)]

    def send(which, src, dst, peer):
        pltpu.make_async_remote_copy(
            src_ref=src, dst_ref=dst,
            send_sem=send_sem.at[which], recv_sem=recv_sem.at[which],
            device_id=peer, device_id_type=MESH,
        ).start()

    load_c = pltpu.make_async_copy(c_hbm, coef, load_sem.at[0])
    load_t = pltpu.make_async_copy(t_hbm, t, load_sem.at[1])
    load_cls = pltpu.make_async_copy(cls_hbm, cls, load_sem.at[2])
    load_e = [pltpu.make_async_copy(
        e_hbm.at[rows_of(k)], e.at[rows_of(k)], load_sem.at[3 + i]) for i, k in enumerate((theirs, core))]
    load_c.start()
    for load in load_e:
        load.start()
    load_t.start()
    load_cls.start()

    barrier = pltpu.get_barrier_semaphore()
    near_z = [dz for k in range(near) for dz in (near - k, k - near)]
    greeted = [*x_mates, *(at_yz(dy, 0) for dy in far_first(ny)), *(at_yz(0, dz) for dz in near_z), other_core]
    for peer in greeted:
        pl.semaphore_signal(barrier, inc=1, device_id=peer, device_id_type=MESH)

    def tell(k, reach):
        for i, dz in enumerate((reach, -reach)):
            pl.semaphore_signal(near_sem.at[2 * k + i], inc=1, device_id=at_yz(0, dz), device_id_type=MESH)

    def hear(k):
        for i in range(2):
            pl.semaphore_wait(near_sem.at[2 * k + i], 1)

    def meet():
        pl.semaphore_wait(barrier, len(greeted))
        tell(0, near)

    def against_rows(left, rows, lanes):
        return lax.dot_general(
            left, e[rows, lanes], (((1,), (1,)), ((), ())), preferred_element_type=F32)

    def x_reduce(which_core, which_x, which_back, buf, product, before_send, between):
        for i, k in enumerate((theirs, core)):
            both = product(rows_of(k), i)
            for j in range(half_tiles):
                part[buf, k * half_tiles + j] = both[:, j * LANES:(j + 1) * LANES]
            if i == 0:
                before_send()
                send(which_core, part.at[buf, tiles_of(k)], crecv.at[buf], other_core)
        between()
        drain(crecv.at[buf], recv_sem.at[which_core])
        xsum[buf, x] = part[buf, tiles_of(core)] + crecv[buf]
        for mate in x_mates:
            send(which_x, xsum.at[buf, x], xsum.at[buf, x], mate)
        drain(xsum.at[buf, pl.ds(0, nx - 1)], recv_sem.at[which_x])
        total = xsum[buf, 0]
        for k in range(1, nx):
            total = total + xsum[buf, k]
        xfull[buf, tiles_of(core)] = total
        send(which_back, xfull.at[buf, tiles_of(core)], xfull.at[buf, tiles_of(core)], other_core)

    def x_halves(which_back, buf, of_tile):
        for i, k in enumerate((core, theirs)):
            if i == 1:
                drain(crecv.at[buf], recv_sem.at[which_back])
            for j in range(half_tiles):
                of_tile(i, k * half_tiles + j)
            if i == 0:
                both = jnp.dot(lhs[:, rows_of(k)], e[rows_of(k), :], preferred_element_type=F32)
                gacc[...] = both[:resp] + both[resp:]

    def y_reduce(which, buf):
        for dy in [*far_first(ny), 0]:
            other = lax.rem(y + dy, ny)
            lanes = pl.ds(pl.multiple_of(other * quarter, quarter), quarter)
            both = jnp.dot(lhs[:, rows_of(theirs)], e[rows_of(theirs), lanes], preferred_element_type=F32)
            total = gacc[:, lanes] + both[:resp] + both[resp:]
            into = ypart.at[buf, other] if dy else yrecv.at[buf, y]
            for p in range(pieces):
                into[p] = total[:, p * LANES:(p + 1) * LANES]
            if dy:
                send(which, ypart.at[buf, other], yrecv.at[buf, y], at_yz(dy, 0))

    def z_reduce(which_y, which_z, buf):
        drain(yrecv.at[buf, pl.ds(0, ny - 1)], recv_sem.at[which_y])
        total = yrecv[buf, 0]
        for k in range(1, ny):
            total = total + yrecv[buf, k]
        ysum[buf] = total
        for dz in far_first(nz):
            peer_piece = lax.rem(z + dz, pieces)
            send(which_z, ysum.at[buf, peer_piece], zrecv.at[buf, z], at_yz(0, dz))
        zrecv[buf, z] = ysum[buf, my_piece]

    def spread_out(which_z, which_g, buf, change):
        drain(zrecv.at[buf, pl.ds(0, nz - 1)], recv_sem.at[which_z])
        total = zrecv[buf, 0]
        for k in range(1, nz):
            total = total + zrecv[buf, k]
        total = change(total)
        gath[buf, y, my_piece] = total
        for dy, dz in spread:
            send(which_g + dy, gath.at[buf, y, my_piece], gath.at[buf, y, my_piece], at_yz(dy, dz))
        return total

    def collect(which_g, buf, dy):
        drain(zrecv.at[buf, pl.ds(0, pieces if dy else pieces - 1)], recv_sem.at[which_g + dy])
        return lax.rem(y - dy + ny, ny)

    by_arrival = [0, *reversed(far_first(ny))]

    lane = lax.broadcasted_iota(jnp.int32, (resp, LANES), 1)
    sub = lax.broadcasted_iota(jnp.int32, (resp, LANES), 0)
    diagonal = lane == sub

    def to_row(column):
        return jnp.sum(jnp.where(diagonal, column, 0.0), axis=0, keepdims=True)

    def to_column(row):
        return jnp.sum(jnp.where(diagonal, row, 0.0), axis=1, keepdims=True)

    load_c.wait()
    cb[...] = coef[...].astype(BF16)

    def first_product(rows, i):
        load_e[i].wait()
        return against_rows(cb[...], rows, slice(None))

    x_reduce(CORE1, X1, BACK1, 0, first_product, meet, lambda: None)
    load_t.wait()
    load_cls.wait()
    hear(0)
    tell(1, 2 * near)

    def put_pair(j, value):
        high = value.astype(BF16)
        low = (value - high.astype(F32)).astype(BF16)
        lhs[0:resp, tile_at(j)] = high
        lhs[resp:2 * resp, tile_at(j)] = low

    def weigh(i, j):
        r = t[:, tile_at(j)] - xfull[0, j]
        resid[j] = r
        norm = jnp.sqrt(jnp.sum(r * r, axis=0, keepdims=True))
        weight = jnp.where(
            cls[pl.ds(j, 1), :] == 1, huber_delta / jnp.maximum(huber_delta, norm), 1.0)
        w[j] = weight
        put_pair(j, weight * r)

    x_halves(BACK1, 0, weigh)

    y_reduce(Y1, 0)
    hear(1)
    z_reduce(Y1, Z1, 0)
    spread_out(Z1, G1, 0, lambda total: total)
    for k, dy in enumerate(by_arrival):
        behind = collect(G1, 0, dy)
        for p in range(pieces):
            lanes = pl.ds(pl.multiple_of(behind * quarter + p * LANES, LANES), LANES)
            piece = gath[0, behind, p]
            g[:, lanes] = piece
            cb[:, lanes] = piece.astype(BF16)
        lanes = pl.ds(pl.multiple_of(behind * quarter, quarter), quarter)
        if k < ny - 1:
            share = against_rows(cb[:, lanes], slice(None), lanes)
            acc[...] = share if k == 0 else acc[...] + share

    def last_product(rows, k):
        return acc[:, rows] + against_rows(cb[:, lanes], rows, lanes)

    def send_gamma():
        norm2 = jnp.zeros((resp, LANES), F32)
        for p in range(ny * pieces):
            piece = g[:, p * LANES:(p + 1) * LANES]
            norm2 = norm2 + piece * piece
        row_x[col] = to_row(jnp.sum(norm2, axis=1, keepdims=True))
        for mate in col_mates:
            send(GAMMA, row_x.at[col], row_x.at[col], mate)

    x_reduce(CORE2, X2, BACK2, 1, last_product, lambda: None, send_gamma)
    curvs = [jnp.zeros((resp, LANES), F32)] * CORES
    weights = [jnp.zeros((1, LANES), F32)] * CORES

    def weigh_image(i, j):
        weight, image = w[j], xfull[1, j]
        scaled = weight * image
        curvs[i] = curvs[i] + scaled * image
        weights[i] = weights[i] + weight
        put_pair(j, scaled)

    x_halves(BACK2, 1, weigh_image)
    curv, weight_sum = curvs[0] + curvs[1], weights[0] + weights[1]
    row_y[y] = to_row(jnp.sum(curv, axis=1, keepdims=True)) + jnp.where(
        lane[0:1] == resp, jnp.sum(weight_sum, axis=1, keepdims=True), 0.0)
    for dy in far_first(ny):
        send(SCAL_Y, row_y.at[y], row_y.at[y], at_yz(dy, 0))

    y_reduce(Y2, 1)
    drain(row_y.at[pl.ds(0, ny - 1)], recv_sem.at[SCAL_Y])
    row_z[z] = jnp.sum(row_y[...], axis=0)
    for dz in far_first(nz):
        send(SCAL_Z, row_z.at[z], row_z.at[z], at_yz(0, dz))
    z_reduce(Y2, Z2, 1)

    drain(row_x.at[pl.ds(0, nc - 1)], recv_sem.at[GAMMA])
    drain(row_z.at[pl.ds(0, nz - 1)], recv_sem.at[SCAL_Z])
    sums = jnp.sum(row_z[...], axis=0)
    gamma_raw = to_column(jnp.sum(row_x[...], axis=0))
    curv_raw = to_column(sums)
    mean = jnp.sum(jnp.where(lane[0:1] == resp, sums, 0.0), axis=1, keepdims=True) / all_rows
    gamma = gamma_raw / (mean * mean)
    alpha = gamma / (curv_raw / (mean * mean * mean))
    ratio = alpha / mean
    coef_out[...] = coef[...] + alpha * (g[...] / mean)
    for j in range(row_tiles):
        resid_out[:, j * LANES:(j + 1) * LANES] = resid[j] - alpha * (xfull[1, j] / mean)

    def piece_of_next(total):
        return g[:, tile_at(y * pieces + my_piece)] - ratio * total

    piece = spread_out(Z2, G2, 1, piece_of_next)
    slot = col * ny * pieces + y * pieces + my_piece
    row_sq[slot] = to_row(jnp.sum(piece * piece, axis=1, keepdims=True))

    def send_square(dc, dy, dz):
        send(SQUARE, row_sq.at[slot], row_sq.at[slot], (at_yz(dy, dz)[0], lax.rem(col + dc, nc)))

    def to_column_block(k, _):
        dc = nc // 2 + lax.div(k + 1, 2) * (2 * lax.rem(k, 2) - 1)
        for dy, dz in [*spread, (0, 0)]:
            send_square(dc, dy, dz)
        return 0

    lax.fori_loop(0, nc - 1, to_column_block, 0)
    for dy, dz in spread:
        send_square(0, dy, dz)
    for dy in by_arrival:
        collect(G2, 1, dy)
    drain(row_sq.at[pl.ds(0, nc * ny * pieces - 1)], recv_sem.at[SQUARE])
    square = to_column(jnp.sum(row_sq[...], axis=0))
    beta = square / (mean * mean) / gamma
    for other in range(ny):
        for p in range(pieces):
            lanes = slice(other * quarter + p * LANES, other * quarter + (p + 1) * LANES)
            dir_out[:, lanes] = gath[1, other, p] / mean + beta * (g[:, lanes] / mean)

    for which, ref in (
        *((which, crecv.at[0]) for which in (CORE1, BACK1, CORE2, BACK2)),
        *((which, xsum.at[0, pl.ds(0, nx - 1)]) for which in (X1, X2)),
        *((which, yrecv.at[0, pl.ds(0, ny - 1)]) for which in (Y1, Y2)),
        *((which, zrecv.at[0, pl.ds(0, nz - 1)]) for which in (Z1, Z2)),
        *((base + k, zrecv.at[0, pl.ds(0, pieces if k else pieces - 1)]) for base in (G1, G2) for k in range(ny)),
        (GAMMA, row_x.at[pl.ds(0, nc - 1)]), (SCAL_Y, row_y.at[pl.ds(0, ny - 1)]), (SCAL_Z, row_z.at[pl.ds(0, nz - 1)]),
        (SQUARE, row_sq.at[pl.ds(0, nc * ny * pieces - 1)]),
    ):
        drain(ref, send_sem.at[which])


def write_out(a_in, b_in, c_in, a_out, b_out, c_out, sems):
    copies = [pltpu.make_async_copy(src, dst, sems.at[k])
              for k, (src, dst) in enumerate(((a_in, a_out), (b_in, b_out), (c_in, c_out)))]
    for copy in copies:
        copy.start()
    for copy in copies:
        copy.wait()


def shards(ny, embeddings, targets, classes, start_coef):
    rows_here, feats = embeddings.shape
    resp = targets.shape[1]
    all_rows = rows_here * lax.axis_size("row")
    nc = lax.axis_size("col")
    nz = lax.axis_size("row") // ny
    row_tiles = rows_here // LANES
    pieces = feats // ny // LANES
    vmem = pltpu.VMEM
    outs = (
        jax.ShapeDtypeStruct((resp, feats), F32),
        jax.ShapeDtypeStruct((resp, rows_here), F32),
        jax.ShapeDtypeStruct((resp, feats), F32),
    )
    results = pl.pallas_call(
        functools.partial(kernel, ny, nz, nc, resp, float(all_rows)),
        out_shape=outs,
        in_specs=[pl.BlockSpec(memory_space=pltpu.HBM)] * 4,
        out_specs=(pl.BlockSpec(memory_space=pltpu.VMEM),) * 3,
        scratch_shapes=[
            vmem((rows_here, feats), BF16),
            vmem((resp, rows_here), F32),
            vmem((row_tiles, LANES), jnp.int32),
            vmem((resp, feats), F32),
            vmem((resp, feats), BF16),
            vmem((resp, rows_here), F32),
            vmem((resp, feats), F32),
            vmem((row_tiles, 1, LANES), F32),
            vmem((row_tiles, resp, LANES), F32),
            vmem((2 * resp, rows_here), BF16),
            vmem((resp, feats), F32),
            vmem((2, row_tiles, resp, LANES), F32),
            vmem((2, row_tiles // CORES, resp, LANES), F32),
            vmem((2, nc // CORES, row_tiles // CORES, resp, LANES), F32),
            vmem((2, row_tiles, resp, LANES), F32),
            vmem((2, ny, pieces, resp, LANES), F32),
            vmem((2, ny, pieces, resp, LANES), F32),
            vmem((2, pieces, resp, LANES), F32),
            vmem((2, max(nz, ny * pieces), resp, LANES), F32),
            vmem((2, ny, pieces, resp, LANES), F32),
            vmem((nc, 1, LANES), F32),
            vmem((ny, 1, LANES), F32),
            vmem((nz, 1, LANES), F32),
            vmem((nc * ny * pieces, 1, LANES), F32),
            pltpu.SemaphoreType.DMA((3 + CORES,)),
            pltpu.SemaphoreType.DMA((N_SEMS,)),
            pltpu.SemaphoreType.DMA((N_SEMS,)),
            pltpu.SemaphoreType.REGULAR((4,)),
        ],
        compiler_params=pltpu.CompilerParams(
            collective_id=0, has_side_effects=True, vmem_limit_bytes=60 * 1024 * 1024),
    )(embeddings, targets.T, classes.reshape(row_tiles, LANES), start_coef.T)
    results = pl.pallas_call(
        write_out,
        out_shape=outs,
        in_specs=[pl.BlockSpec(memory_space=pltpu.VMEM)] * 3,
        out_specs=(pl.BlockSpec(memory_space=pl.ANY),) * 3,
        scratch_shapes=[pltpu.SemaphoreType.DMA((3,))],
        compiler_params=pltpu.CompilerParams(vmem_limit_bytes=60 * 1024 * 1024),
    )(*results)
    return tuple(out.T for out in results)


def solution(mesh, y_chips=Y_CHIPS):
    return jax.shard_map(
        functools.partial(shards, y_chips),
        mesh=mesh,
        in_specs=(P("row", "col"), P("row", None), P("row"), P("col", None)),
        out_specs=(P("col", None), P("row", None), P("col", None)),
        check_vma=False,
    )
```

```python
import functools

import jax
import jax.numpy as jnp
from jax import lax
from jax.experimental import pallas as pl
from jax.experimental.pallas import tpu as pltpu
from jax.sharding import PartitionSpec as P

MESH = pl.DeviceIdType.MESH
BF16 = jnp.bfloat16
F32 = jnp.float32
huber_delta = 8.0
LANES = 128
Y_CHIPS = 4
CORES = 2

(CORE1, X1, BACK1, Y1, Z1, GAMMA, CORE2, X2, BACK2, SCAL_Y, SCAL_Z, Y2, Z2, SQUARE, G1) = range(15)
G2 = G1 + Y_CHIPS
N_SEMS = G2 + Y_CHIPS


def drain(ref, sem):
    pltpu.make_async_copy(ref, ref, sem).wait()


def kernel(ny, nz, nc, resp, all_rows,
           e_hbm, t_hbm, cls_hbm, c_hbm,
           coef_out, resid_out, dir_out,
           e, t, cls, coef, cb, acc, gacc, w, resid, lhs, g,
           part, crecv, xsum, xfull, yrecv, ypart, ysum, zrecv, gath,
           row_x, row_y, row_z, row_sq,
           load_sem, send_sem, recv_sem, near_sem):
    rows_here, feats = e.shape
    row_tiles = rows_here // LANES
    half_rows = rows_here // CORES
    half_tiles = row_tiles // CORES
    quarter = feats // ny
    pieces = quarter // LANES
    nx = nc // CORES
    near = nz // 8
    here = lax.axis_index("row")
    col = lax.axis_index("col")
    y, z = lax.div(here, nz), lax.rem(here, nz)
    x, core = lax.div(col, CORES), lax.rem(col, CORES)
    my_piece = lax.rem(z, pieces)
    theirs = 1 - core

    def tile_at(j):
        return pl.ds(pl.multiple_of(j * LANES, LANES), LANES)

    def rows_of(k):
        return pl.ds(pl.multiple_of(k * half_rows, half_rows), half_rows)

    def tiles_of(k):
        return pl.ds(k * half_tiles, half_tiles)

    def far_first(n):
        return [n // 2 + ((k + 1) // 2) * (2 * (k % 2) - 1) for k in range(n - 1)]

    def at_yz(dy, dz):
        return lax.rem(y + dy + ny, ny) * nz + lax.rem(z + dz + nz, nz), col

    def at_col(dc):
        return here, lax.rem(col + dc, nc)

    other_core = (here, col + 1 - 2 * core)
    x_mates = [(here, lax.rem(x + dx, nx) * CORES + core) for dx in far_first(nx)]
    col_mates = [at_col(dc) for dc in far_first(nc)]
    spread = [(dy, dz) for dz in sorted(range(1 - pieces // 2, pieces // 2 + 1), key=lambda d: -abs(d))
              for dy in [*far_first(ny), 0] if (dy, dz) != (0, 0)]

    def send(which, src, dst, peer):
        pltpu.make_async_remote_copy(
            src_ref=src, dst_ref=dst,
            send_sem=send_sem.at[which], recv_sem=recv_sem.at[which],
            device_id=peer, device_id_type=MESH,
        ).start()

    load_c = pltpu.make_async_copy(c_hbm, coef, load_sem.at[0])
    load_t = pltpu.make_async_copy(t_hbm, t, load_sem.at[1])
    load_cls = pltpu.make_async_copy(cls_hbm, cls, load_sem.at[2])
    load_e = [pltpu.make_async_copy(
        e_hbm.at[rows_of(k)], e.at[rows_of(k)], load_sem.at[3 + i]) for i, k in enumerate((theirs, core))]
    load_c.start()
    for load in load_e:
        load.start()
    load_t.start()
    load_cls.start()

    barrier = pltpu.get_barrier_semaphore()
    near_z = [dz for k in range(near) for dz in (near - k, k - near)]
    greeted = [*x_mates, *(at_yz(dy, 0) for dy in far_first(ny)), *(at_yz(0, dz) for dz in near_z), other_core]
    for peer in greeted:
        pl.semaphore_signal(barrier, inc=1, device_id=peer, device_id_type=MESH)

    def tell(k, reach):
        for i, dz in enumerate((reach, -reach)):
            pl.semaphore_signal(near_sem.at[2 * k + i], inc=1, device_id=at_yz(0, dz), device_id_type=MESH)

    def hear(k):
        for i in range(2):
            pl.semaphore_wait(near_sem.at[2 * k + i], 1)

    def meet():
        pl.semaphore_wait(barrier, len(greeted))
        tell(0, near)

    def against_rows(left, rows, lanes):
        return lax.dot_general(
            left, e[rows, lanes], (((1,), (1,)), ((), ())), preferred_element_type=F32)

    def x_reduce(which_core, which_x, which_back, buf, product, before_send, between):
        for i, k in enumerate((theirs, core)):
            both = product(rows_of(k), i)
            for j in range(half_tiles):
                part[buf, k * half_tiles + j] = both[:, j * LANES:(j + 1) * LANES]
            if i == 0:
                before_send()
                send(which_core, part.at[buf, tiles_of(k)], crecv.at[buf], other_core)
        between()
        drain(crecv.at[buf], recv_sem.at[which_core])
        xsum[buf, x] = part[buf, tiles_of(core)] + crecv[buf]
        for mate in x_mates:
            send(which_x, xsum.at[buf, x], xsum.at[buf, x], mate)
        drain(xsum.at[buf, pl.ds(0, nx - 1)], recv_sem.at[which_x])
        total = xsum[buf, 0]
        for k in range(1, nx):
            total = total + xsum[buf, k]
        xfull[buf, tiles_of(core)] = total
        send(which_back, xfull.at[buf, tiles_of(core)], xfull.at[buf, tiles_of(core)], other_core)

    def x_halves(which_back, buf, of_half):
        for i, k in enumerate((core, theirs)):
            if i == 1:
                drain(crecv.at[buf], recv_sem.at[which_back])
            of_half(i, k)
            if i == 0:
                both = jnp.dot(lhs[:, rows_of(k)], e[rows_of(k), :], preferred_element_type=F32)
                gacc[...] = both[:resp] + both[resp:]

    def y_reduce(which, buf):
        for dy in [*far_first(ny), 0]:
            other = lax.rem(y + dy, ny)
            lanes = pl.ds(pl.multiple_of(other * quarter, quarter), quarter)
            both = jnp.dot(lhs[:, rows_of(theirs)], e[rows_of(theirs), lanes], preferred_element_type=F32)
            total = gacc[:, lanes] + both[:resp] + both[resp:]
            into = ypart.at[buf, other] if dy else yrecv.at[buf, y]
            for p in range(pieces):
                into[p] = total[:, p * LANES:(p + 1) * LANES]
            if dy:
                send(which, ypart.at[buf, other], yrecv.at[buf, y], at_yz(dy, 0))

    def z_reduce(which_y, which_z, buf):
        drain(yrecv.at[buf, pl.ds(0, ny - 1)], recv_sem.at[which_y])
        total = yrecv[buf, 0]
        for k in range(1, ny):
            total = total + yrecv[buf, k]
        ysum[buf] = total
        for dz in far_first(nz):
            peer_piece = lax.rem(z + dz, pieces)
            send(which_z, ysum.at[buf, peer_piece], zrecv.at[buf, z], at_yz(0, dz))
        zrecv[buf, z] = ysum[buf, my_piece]

    def spread_out(which_z, which_g, buf, change, first=lambda total: None):
        drain(zrecv.at[buf, pl.ds(0, nz - 1)], recv_sem.at[which_z])
        total = zrecv[buf, 0]
        for k in range(1, nz):
            total = total + zrecv[buf, k]
        total = change(total)
        gath[buf, y, my_piece] = total
        first(total)
        for dy, dz in spread:
            send(which_g + dy, gath.at[buf, y, my_piece], gath.at[buf, y, my_piece], at_yz(dy, dz))
        return total

    def collect(which_g, buf, dy):
        drain(zrecv.at[buf, pl.ds(0, pieces if dy else pieces - 1)], recv_sem.at[which_g + dy])
        return lax.rem(y - dy + ny, ny)

    by_arrival = [0, *reversed(far_first(ny))]

    lane = lax.broadcasted_iota(jnp.int32, (resp, LANES), 1)
    sub = lax.broadcasted_iota(jnp.int32, (resp, LANES), 0)
    diagonal = lane == sub

    def to_row(column):
        return jnp.sum(jnp.where(diagonal, column, 0.0), axis=0, keepdims=True)

    def to_column(row):
        return jnp.sum(jnp.where(diagonal, row, 0.0), axis=1, keepdims=True)

    load_c.wait()
    cb[...] = coef[...].astype(BF16)

    def first_product(rows, i):
        load_e[i].wait()
        return against_rows(cb[...], rows, slice(None))

    x_reduce(CORE1, X1, BACK1, 0, first_product, meet, lambda: None)
    load_t.wait()
    load_cls.wait()
    hear(0)
    tell(1, 2 * near)

    def put_pairs(k, values):
        for j, value in enumerate(values):
            high = value.astype(BF16)
            lhs[0:resp, tile_at(k * half_tiles + j)] = high
            lhs[resp:2 * resp, tile_at(k * half_tiles + j)] = (value - high.astype(F32)).astype(BF16)

    def weigh(i, k):
        rs = [t[:, tile_at(k * half_tiles + j)] - xfull[0, k * half_tiles + j] for j in range(half_tiles)]
        norm = jnp.sqrt(jnp.concatenate([jnp.sum(r * r, axis=0, keepdims=True) for r in rs], axis=0))
        huber = jnp.where(k == 0, cls[0:half_tiles], cls[half_tiles:2 * half_tiles]) == 1
        weight = jnp.where(huber, huber_delta / jnp.maximum(huber_delta, norm), 1.0)
        put_pairs(k, [weight[j:j + 1] * r for j, r in enumerate(rs)])
        w[k] = weight
        for j, r in enumerate(rs):
            resid[k * half_tiles + j] = r

    x_halves(BACK1, 0, weigh)

    y_reduce(Y1, 0)
    hear(1)
    z_reduce(Y1, Z1, 0)
    spread_out(Z1, G1, 0, lambda total: total)
    for k, dy in enumerate(by_arrival):
        behind = collect(G1, 0, dy)
        for p in range(pieces):
            lanes = pl.ds(pl.multiple_of(behind * quarter + p * LANES, LANES), LANES)
            piece = gath[0, behind, p]
            g[:, lanes] = piece
            cb[:, lanes] = piece.astype(BF16)
        lanes = pl.ds(pl.multiple_of(behind * quarter, quarter), quarter)
        if k < ny - 1:
            share = against_rows(cb[:, lanes], slice(None), lanes)
            acc[...] = share if k == 0 else acc[...] + share

    def last_product(rows, k):
        return acc[:, rows] + against_rows(cb[:, lanes], rows, lanes)

    def send_gamma():
        norm2 = jnp.zeros((resp, LANES), F32)
        for p in range(ny * pieces):
            piece = g[:, p * LANES:(p + 1) * LANES]
            norm2 = norm2 + piece * piece
        row_x[col] = to_row(jnp.sum(norm2, axis=1, keepdims=True))
        for mate in col_mates:
            send(GAMMA, row_x.at[col], row_x.at[col], mate)

    x_reduce(CORE2, X2, BACK2, 1, last_product, lambda: None, send_gamma)
    curvs = [jnp.zeros((resp, LANES), F32)] * CORES
    weights = [None] * CORES

    def weigh_image(i, k):
        weight = w[k]
        images = [xfull[1, k * half_tiles + j] for j in range(half_tiles)]
        scaled = [weight[j:j + 1] * image for j, image in enumerate(images)]
        put_pairs(k, scaled)
        for j, image in enumerate(images):
            curvs[i] = curvs[i] + scaled[j] * image
        weights[i] = jnp.sum(weight, axis=0, keepdims=True)

    x_halves(BACK2, 1, weigh_image)
    curv, weight_sum = curvs[0] + curvs[1], weights[0] + weights[1]
    row_y[y] = to_row(jnp.sum(curv, axis=1, keepdims=True)) + jnp.where(
        lane[0:1] == resp, jnp.sum(weight_sum, axis=1, keepdims=True), 0.0)
    for dy in far_first(ny):
        send(SCAL_Y, row_y.at[y], row_y.at[y], at_yz(dy, 0))

    y_reduce(Y2, 1)
    drain(row_y.at[pl.ds(0, ny - 1)], recv_sem.at[SCAL_Y])
    row_z[z] = jnp.sum(row_y[...], axis=0)
    for dz in far_first(nz):
        send(SCAL_Z, row_z.at[z], row_z.at[z], at_yz(0, dz))
    z_reduce(Y2, Z2, 1)

    drain(row_x.at[pl.ds(0, nc - 1)], recv_sem.at[GAMMA])
    drain(row_z.at[pl.ds(0, nz - 1)], recv_sem.at[SCAL_Z])
    sums = jnp.sum(row_z[...], axis=0)
    gamma_raw = to_column(jnp.sum(row_x[...], axis=0))
    curv_raw = to_column(sums)
    mean = jnp.sum(jnp.where(lane[0:1] == resp, sums, 0.0), axis=1, keepdims=True) / all_rows
    gamma = gamma_raw / (mean * mean)
    alpha = gamma / (curv_raw / (mean * mean * mean))
    ratio = alpha / mean
    coef_out[...] = coef[...] + alpha * (g[...] / mean)
    for j in range(row_tiles):
        resid_out[:, j * LANES:(j + 1) * LANES] = resid[j] - alpha * (xfull[1, j] / mean)

    def piece_of_next(total):
        return g[:, tile_at(y * pieces + my_piece)] - ratio * total

    slot = col * ny * pieces + y * pieces + my_piece

    def send_square(dc, dy, dz):
        send(SQUARE, row_sq.at[slot], row_sq.at[slot], (at_yz(dy, dz)[0], lax.rem(col + dc, nc)))

    def to_column_block(k, _):
        dc = nc // 2 + lax.div(k + 1, 2) * (2 * lax.rem(k, 2) - 1)
        for dy, dz in [*spread, (0, 0)]:
            send_square(dc, dy, dz)
        return 0

    def send_squares(piece):
        row_sq[slot] = to_row(jnp.sum(piece * piece, axis=1, keepdims=True))
        lax.fori_loop(0, nc - 1, to_column_block, 0)
        for dy, dz in spread:
            send_square(0, dy, dz)

    spread_out(Z2, G2, 1, piece_of_next, send_squares)
    for dy in by_arrival:
        collect(G2, 1, dy)
    drain(row_sq.at[pl.ds(0, nc * ny * pieces - 1)], recv_sem.at[SQUARE])
    square = to_column(jnp.sum(row_sq[...], axis=0))
    beta = square / (mean * mean) / gamma
    for other in range(ny):
        for p in range(pieces):
            lanes = slice(other * quarter + p * LANES, other * quarter + (p + 1) * LANES)
            dir_out[:, lanes] = gath[1, other, p] / mean + beta * (g[:, lanes] / mean)

    for which, ref in (
        *((which, crecv.at[0]) for which in (CORE1, BACK1, CORE2, BACK2)),
        *((which, xsum.at[0, pl.ds(0, nx - 1)]) for which in (X1, X2)),
        *((which, yrecv.at[0, pl.ds(0, ny - 1)]) for which in (Y1, Y2)),
        *((which, zrecv.at[0, pl.ds(0, nz - 1)]) for which in (Z1, Z2)),
        *((base + k, zrecv.at[0, pl.ds(0, pieces if k else pieces - 1)]) for base in (G1, G2) for k in range(ny)),
        (GAMMA, row_x.at[pl.ds(0, nc - 1)]), (SCAL_Y, row_y.at[pl.ds(0, ny - 1)]), (SCAL_Z, row_z.at[pl.ds(0, nz - 1)]),
        (SQUARE, row_sq.at[pl.ds(0, nc * ny * pieces - 1)]),
    ):
        drain(ref, send_sem.at[which])


def write_out(a_in, b_in, c_in, a_out, b_out, c_out, sems):
    copies = [pltpu.make_async_copy(src, dst, sems.at[k])
              for k, (src, dst) in enumerate(((a_in, a_out), (b_in, b_out), (c_in, c_out)))]
    for copy in copies:
        copy.start()
    for copy in copies:
        copy.wait()


def shards(ny, embeddings, targets, classes, start_coef):
    rows_here, feats = embeddings.shape
    resp = targets.shape[1]
    all_rows = rows_here * lax.axis_size("row")
    nc = lax.axis_size("col")
    nz = lax.axis_size("row") // ny
    row_tiles = rows_here // LANES
    pieces = feats // ny // LANES
    vmem = pltpu.VMEM
    outs = (
        jax.ShapeDtypeStruct((resp, feats), F32),
        jax.ShapeDtypeStruct((resp, rows_here), F32),
        jax.ShapeDtypeStruct((resp, feats), F32),
    )
    results = pl.pallas_call(
        functools.partial(kernel, ny, nz, nc, resp, float(all_rows)),
        out_shape=outs,
        in_specs=[pl.BlockSpec(memory_space=pltpu.HBM)] * 4,
        out_specs=(pl.BlockSpec(memory_space=pltpu.VMEM),) * 3,
        scratch_shapes=[
            vmem((rows_here, feats), BF16),
            vmem((resp, rows_here), F32),
            vmem((row_tiles, LANES), jnp.int32),
            vmem((resp, feats), F32),
            vmem((resp, feats), BF16),
            vmem((resp, rows_here), F32),
            vmem((resp, feats), F32),
            vmem((CORES, row_tiles // CORES, LANES), F32),
            vmem((row_tiles, resp, LANES), F32),
            vmem((2 * resp, rows_here), BF16),
            vmem((resp, feats), F32),
            vmem((2, row_tiles, resp, LANES), F32),
            vmem((2, row_tiles // CORES, resp, LANES), F32),
            vmem((2, nc // CORES, row_tiles // CORES, resp, LANES), F32),
            vmem((2, row_tiles, resp, LANES), F32),
            vmem((2, ny, pieces, resp, LANES), F32),
            vmem((2, ny, pieces, resp, LANES), F32),
            vmem((2, pieces, resp, LANES), F32),
            vmem((2, max(nz, ny * pieces), resp, LANES), F32),
            vmem((2, ny, pieces, resp, LANES), F32),
            vmem((nc, 1, LANES), F32),
            vmem((ny, 1, LANES), F32),
            vmem((nz, 1, LANES), F32),
            vmem((nc * ny * pieces, 1, LANES), F32),
            pltpu.SemaphoreType.DMA((3 + CORES,)),
            pltpu.SemaphoreType.DMA((N_SEMS,)),
            pltpu.SemaphoreType.DMA((N_SEMS,)),
            pltpu.SemaphoreType.REGULAR((4,)),
        ],
        compiler_params=pltpu.CompilerParams(
            collective_id=0, has_side_effects=True, vmem_limit_bytes=60 * 1024 * 1024),
    )(embeddings, targets.T, classes.reshape(row_tiles, LANES), start_coef.T)
    results = pl.pallas_call(
        write_out,
        out_shape=outs,
        in_specs=[pl.BlockSpec(memory_space=pltpu.VMEM)] * 3,
        out_specs=(pl.BlockSpec(memory_space=pl.ANY),) * 3,
        scratch_shapes=[pltpu.SemaphoreType.DMA((3,))],
        compiler_params=pltpu.CompilerParams(vmem_limit_bytes=60 * 1024 * 1024),
    )(*results)
    return tuple(out.T for out in results)


def solution(mesh, y_chips=Y_CHIPS):
    return jax.shard_map(
        functools.partial(shards, y_chips),
        mesh=mesh,
        in_specs=(P("row", "col"), P("row", None), P("row"), P("col", None)),
        out_specs=(P("col", None), P("row", None), P("col", None)),
        check_vma=False,
    )
```

```python
import functools

import jax
import jax.numpy as jnp
from jax import lax
from jax.experimental import pallas as pl
from jax.experimental.pallas import tpu as pltpu
from jax.sharding import PartitionSpec as P

MESH = pl.DeviceIdType.MESH
BF16 = jnp.bfloat16
F32 = jnp.float32
huber_delta = 8.0
LANES = 128
Y_CHIPS = 4
CORES = 2

(CORE1, X1, BACK1, Y1, Z1, GAMMA, CORE2, X2, BACK2, SCAL_Y, SCAL_Z, Y2, Z2, SQUARE, G1) = range(15)
G2 = G1 + Y_CHIPS
N_SEMS = G2 + Y_CHIPS


def drain(ref, sem):
    pltpu.make_async_copy(ref, ref, sem).wait()


def kernel(ny, nz, nc, resp, all_rows,
           e_hbm, t_hbm, cls_hbm, c_hbm,
           coef_hbm, resid_hbm, dir_hbm,
           coef_out, resid_out, dir_out,
           e, t, cls, coef, cb, acc, gacc, w, resid, lhs, g,
           part, crecv, xsum, xfull, yrecv, ypart, ysum, zrecv, gath,
           row_x, row_y, row_z, row_sq,
           load_sem, send_sem, recv_sem, near_sem, out_sem):
    rows_here, feats = e.shape
    row_tiles = rows_here // LANES
    half_rows = rows_here // CORES
    half_tiles = row_tiles // CORES
    quarter = feats // ny
    pieces = quarter // LANES
    nx = nc // CORES
    near = nz // 8
    here = lax.axis_index("row")
    col = lax.axis_index("col")
    y, z = lax.div(here, nz), lax.rem(here, nz)
    x, core = lax.div(col, CORES), lax.rem(col, CORES)
    my_piece = lax.rem(z, pieces)
    theirs = 1 - core

    def tile_at(j):
        return pl.ds(pl.multiple_of(j * LANES, LANES), LANES)

    def rows_of(k):
        return pl.ds(pl.multiple_of(k * half_rows, half_rows), half_rows)

    def tiles_of(k):
        return pl.ds(k * half_tiles, half_tiles)

    def far_first(n):
        return [n // 2 + ((k + 1) // 2) * (2 * (k % 2) - 1) for k in range(n - 1)]

    def at_yz(dy, dz):
        return lax.rem(y + dy + ny, ny) * nz + lax.rem(z + dz + nz, nz), col

    def at_col(dc):
        return here, lax.rem(col + dc, nc)

    other_core = (here, col + 1 - 2 * core)
    x_mates = [(here, lax.rem(x + dx, nx) * CORES + core) for dx in far_first(nx)]
    col_mates = [at_col(dc) for dc in far_first(nc)]
    spread = [(dy, dz) for dz in sorted(range(1 - pieces // 2, pieces // 2 + 1), key=lambda d: -abs(d))
              for dy in [*far_first(ny), 0] if (dy, dz) != (0, 0)]

    def send(which, src, dst, peer):
        pltpu.make_async_remote_copy(
            src_ref=src, dst_ref=dst,
            send_sem=send_sem.at[which], recv_sem=recv_sem.at[which],
            device_id=peer, device_id_type=MESH,
        ).start()

    load_c = pltpu.make_async_copy(c_hbm, coef, load_sem.at[0])
    load_t = pltpu.make_async_copy(t_hbm, t, load_sem.at[1])
    load_cls = pltpu.make_async_copy(cls_hbm, cls, load_sem.at[2])
    load_e = [pltpu.make_async_copy(
        e_hbm.at[rows_of(k)], e.at[rows_of(k)], load_sem.at[3 + i]) for i, k in enumerate((theirs, core))]
    load_c.start()
    for load in load_e:
        load.start()
    load_t.start()
    load_cls.start()

    barrier = pltpu.get_barrier_semaphore()
    near_z = [dz for k in range(near) for dz in (near - k, k - near)]
    greeted = [*x_mates, *(at_yz(dy, 0) for dy in far_first(ny)), *(at_yz(0, dz) for dz in near_z), other_core]
    for peer in greeted:
        pl.semaphore_signal(barrier, inc=1, device_id=peer, device_id_type=MESH)

    def tell(k, reach):
        for i, dz in enumerate((reach, -reach)):
            pl.semaphore_signal(near_sem.at[2 * k + i], inc=1, device_id=at_yz(0, dz), device_id_type=MESH)

    def hear(k):
        for i in range(2):
            pl.semaphore_wait(near_sem.at[2 * k + i], 1)

    def meet():
        pl.semaphore_wait(barrier, len(greeted))
        tell(0, near)

    def against_rows(left, rows, lanes):
        return lax.dot_general(
            left, e[rows, lanes], (((1,), (1,)), ((), ())), preferred_element_type=F32)

    def x_reduce(which_core, which_x, which_back, buf, product, before_send, between):
        for i, k in enumerate((theirs, core)):
            both = product(rows_of(k), i)
            for j in range(half_tiles):
                part[buf, k * half_tiles + j] = both[:, j * LANES:(j + 1) * LANES]
            if i == 0:
                before_send()
                send(which_core, part.at[buf, tiles_of(k)], crecv.at[buf], other_core)
        between()
        drain(crecv.at[buf], recv_sem.at[which_core])
        xsum[buf, x] = part[buf, tiles_of(core)] + crecv[buf]
        for mate in x_mates:
            send(which_x, xsum.at[buf, x], xsum.at[buf, x], mate)
        drain(xsum.at[buf, pl.ds(0, nx - 1)], recv_sem.at[which_x])
        total = xsum[buf, 0]
        for k in range(1, nx):
            total = total + xsum[buf, k]
        xfull[buf, tiles_of(core)] = total
        send(which_back, xfull.at[buf, tiles_of(core)], xfull.at[buf, tiles_of(core)], other_core)

    def x_halves(which_back, buf, of_half):
        for i, k in enumerate((core, theirs)):
            if i == 1:
                drain(crecv.at[buf], recv_sem.at[which_back])
            of_half(i, k)
            if i == 0:
                both = jnp.dot(lhs[:, rows_of(k)], e[rows_of(k), :], preferred_element_type=F32)
                gacc[...] = both[:resp] + both[resp:]

    def y_reduce(which, buf):
        for dy in [*far_first(ny), 0]:
            other = lax.rem(y + dy, ny)
            lanes = pl.ds(pl.multiple_of(other * quarter, quarter), quarter)
            both = jnp.dot(lhs[:, rows_of(theirs)], e[rows_of(theirs), lanes], preferred_element_type=F32)
            total = gacc[:, lanes] + both[:resp] + both[resp:]
            into = ypart.at[buf, other] if dy else yrecv.at[buf, y]
            for p in range(pieces):
                into[p] = total[:, p * LANES:(p + 1) * LANES]
            if dy:
                send(which, ypart.at[buf, other], yrecv.at[buf, y], at_yz(dy, 0))

    def z_reduce(which_y, which_z, buf):
        drain(yrecv.at[buf, pl.ds(0, ny - 1)], recv_sem.at[which_y])
        total = yrecv[buf, 0]
        for k in range(1, ny):
            total = total + yrecv[buf, k]
        ysum[buf] = total
        for dz in far_first(nz):
            peer_piece = lax.rem(z + dz, pieces)
            send(which_z, ysum.at[buf, peer_piece], zrecv.at[buf, z], at_yz(0, dz))
        zrecv[buf, z] = ysum[buf, my_piece]

    def spread_out(which_z, which_g, buf, change, first=lambda total: None):
        drain(zrecv.at[buf, pl.ds(0, nz - 1)], recv_sem.at[which_z])
        total = zrecv[buf, 0]
        for k in range(1, nz):
            total = total + zrecv[buf, k]
        total = change(total)
        gath[buf, y, my_piece] = total
        first(total)
        for dy, dz in spread:
            send(which_g + dy, gath.at[buf, y, my_piece], gath.at[buf, y, my_piece], at_yz(dy, dz))
        return total

    def collect(which_g, buf, dy):
        drain(zrecv.at[buf, pl.ds(0, pieces if dy else pieces - 1)], recv_sem.at[which_g + dy])
        return lax.rem(y - dy + ny, ny)

    by_arrival = [0, *reversed(far_first(ny))]

    lane = lax.broadcasted_iota(jnp.int32, (resp, LANES), 1)
    sub = lax.broadcasted_iota(jnp.int32, (resp, LANES), 0)
    diagonal = lane == sub

    def to_row(column):
        return jnp.sum(jnp.where(diagonal, column, 0.0), axis=0, keepdims=True)

    def to_column(row):
        return jnp.sum(jnp.where(diagonal, row, 0.0), axis=1, keepdims=True)

    load_c.wait()
    cb[...] = coef[...].astype(BF16)

    def first_product(rows, i):
        load_e[i].wait()
        return against_rows(cb[...], rows, slice(None))

    x_reduce(CORE1, X1, BACK1, 0, first_product, meet, lambda: None)
    load_t.wait()
    load_cls.wait()
    hear(0)
    tell(1, 2 * near)

    def put_pairs(k, values):
        for j, value in enumerate(values):
            high = value.astype(BF16)
            lhs[0:resp, tile_at(k * half_tiles + j)] = high
            lhs[resp:2 * resp, tile_at(k * half_tiles + j)] = (value - high.astype(F32)).astype(BF16)

    def weigh(i, k):
        rs = [t[:, tile_at(k * half_tiles + j)] - xfull[0, k * half_tiles + j] for j in range(half_tiles)]
        norm = jnp.sqrt(jnp.concatenate([jnp.sum(r * r, axis=0, keepdims=True) for r in rs], axis=0))
        huber = jnp.where(k == 0, cls[0:half_tiles], cls[half_tiles:2 * half_tiles]) == 1
        weight = jnp.where(huber, huber_delta / jnp.maximum(huber_delta, norm), 1.0)
        put_pairs(k, [weight[j:j + 1] * r for j, r in enumerate(rs)])
        w[k] = weight
        for j, r in enumerate(rs):
            resid[k * half_tiles + j] = r

    x_halves(BACK1, 0, weigh)

    y_reduce(Y1, 0)
    hear(1)
    z_reduce(Y1, Z1, 0)
    spread_out(Z1, G1, 0, lambda total: total)
    for k, dy in enumerate(by_arrival):
        behind = collect(G1, 0, dy)
        for p in range(pieces):
            lanes = pl.ds(pl.multiple_of(behind * quarter + p * LANES, LANES), LANES)
            piece = gath[0, behind, p]
            g[:, lanes] = piece
            cb[:, lanes] = piece.astype(BF16)
        lanes = pl.ds(pl.multiple_of(behind * quarter, quarter), quarter)
        if k < ny - 1:
            share = against_rows(cb[:, lanes], slice(None), lanes)
            acc[...] = share if k == 0 else acc[...] + share

    def last_product(rows, k):
        return acc[:, rows] + against_rows(cb[:, lanes], rows, lanes)

    def send_gamma():
        norm2 = jnp.zeros((resp, LANES), F32)
        for p in range(ny * pieces):
            piece = g[:, p * LANES:(p + 1) * LANES]
            norm2 = norm2 + piece * piece
        row_x[col] = to_row(jnp.sum(norm2, axis=1, keepdims=True))
        for mate in col_mates:
            send(GAMMA, row_x.at[col], row_x.at[col], mate)

    x_reduce(CORE2, X2, BACK2, 1, last_product, lambda: None, send_gamma)
    curvs = [jnp.zeros((resp, LANES), F32)] * CORES
    weights = [None] * CORES

    def weigh_image(i, k):
        weight = w[k]
        images = [xfull[1, k * half_tiles + j] for j in range(half_tiles)]
        scaled = [weight[j:j + 1] * image for j, image in enumerate(images)]
        put_pairs(k, scaled)
        for j, image in enumerate(images):
            curvs[i] = curvs[i] + scaled[j] * image
        weights[i] = jnp.sum(weight, axis=0, keepdims=True)

    x_halves(BACK2, 1, weigh_image)
    curv, weight_sum = curvs[0] + curvs[1], weights[0] + weights[1]
    row_y[y] = to_row(jnp.sum(curv, axis=1, keepdims=True)) + jnp.where(
        lane[0:1] == resp, jnp.sum(weight_sum, axis=1, keepdims=True), 0.0)
    for dy in far_first(ny):
        send(SCAL_Y, row_y.at[y], row_y.at[y], at_yz(dy, 0))

    y_reduce(Y2, 1)
    drain(row_y.at[pl.ds(0, ny - 1)], recv_sem.at[SCAL_Y])
    row_z[z] = jnp.sum(row_y[...], axis=0)
    for dz in far_first(nz):
        send(SCAL_Z, row_z.at[z], row_z.at[z], at_yz(0, dz))
    z_reduce(Y2, Z2, 1)

    drain(row_x.at[pl.ds(0, nc - 1)], recv_sem.at[GAMMA])
    drain(row_z.at[pl.ds(0, nz - 1)], recv_sem.at[SCAL_Z])
    sums = jnp.sum(row_z[...], axis=0)
    gamma_raw = to_column(jnp.sum(row_x[...], axis=0))
    curv_raw = to_column(sums)
    mean = jnp.sum(jnp.where(lane[0:1] == resp, sums, 0.0), axis=1, keepdims=True) / all_rows
    gamma = gamma_raw / (mean * mean)
    alpha = gamma / (curv_raw / (mean * mean * mean))
    ratio = alpha / mean
    coef_out[...] = coef[...] + alpha * (g[...] / mean)
    for j in range(row_tiles):
        resid_out[:, j * LANES:(j + 1) * LANES] = resid[j] - alpha * (xfull[1, j] / mean)
    stores = [pltpu.make_async_copy(src, dst, out_sem.at[k]) for k, (src, dst) in enumerate(
        ((coef_out, coef_hbm), (resid_out, resid_hbm), (dir_out, dir_hbm)))]
    stores[0].start()
    stores[1].start()

    def piece_of_next(total):
        return g[:, tile_at(y * pieces + my_piece)] - ratio * total

    slot = col * ny * pieces + y * pieces + my_piece

    def send_square(dc, dy, dz):
        send(SQUARE, row_sq.at[slot], row_sq.at[slot], (at_yz(dy, dz)[0], lax.rem(col + dc, nc)))

    def to_column_block(k, _):
        dc = nc // 2 + lax.div(k + 1, 2) * (2 * lax.rem(k, 2) - 1)
        for dy, dz in [*spread, (0, 0)]:
            send_square(dc, dy, dz)
        return 0

    def send_squares(piece):
        row_sq[slot] = to_row(jnp.sum(piece * piece, axis=1, keepdims=True))
        lax.fori_loop(0, nc - 1, to_column_block, 0)
        for dy, dz in spread:
            send_square(0, dy, dz)

    spread_out(Z2, G2, 1, piece_of_next, send_squares)
    for dy in by_arrival:
        collect(G2, 1, dy)
    drain(row_sq.at[pl.ds(0, nc * ny * pieces - 1)], recv_sem.at[SQUARE])
    square = to_column(jnp.sum(row_sq[...], axis=0))
    beta = square / (mean * mean) / gamma
    for other in range(ny):
        for p in range(pieces):
            lanes = slice(other * quarter + p * LANES, other * quarter + (p + 1) * LANES)
            dir_out[:, lanes] = gath[1, other, p] / mean + beta * (g[:, lanes] / mean)
    stores[2].start()

    for which, ref in (
        *((which, crecv.at[0]) for which in (CORE1, BACK1, CORE2, BACK2)),
        *((which, xsum.at[0, pl.ds(0, nx - 1)]) for which in (X1, X2)),
        *((which, yrecv.at[0, pl.ds(0, ny - 1)]) for which in (Y1, Y2)),
        *((which, zrecv.at[0, pl.ds(0, nz - 1)]) for which in (Z1, Z2)),
        *((base + k, zrecv.at[0, pl.ds(0, pieces if k else pieces - 1)]) for base in (G1, G2) for k in range(ny)),
        (GAMMA, row_x.at[pl.ds(0, nc - 1)]), (SCAL_Y, row_y.at[pl.ds(0, ny - 1)]), (SCAL_Z, row_z.at[pl.ds(0, nz - 1)]),
        (SQUARE, row_sq.at[pl.ds(0, nc * ny * pieces - 1)]),
    ):
        drain(ref, send_sem.at[which])
    for store in stores:
        store.wait()


def write_out(a_in, b_in, c_in, a_out, b_out, c_out, a, b, c, sems):
    moves = ((a_in, a, a_out), (b_in, b, b_out), (c_in, c, c_out))
    loads = [pltpu.make_async_copy(src, held, sems.at[0, k]) for k, (src, held, _) in enumerate(moves)]
    stores = [pltpu.make_async_copy(held, dst, sems.at[1, k]) for k, (_, held, dst) in enumerate(moves)]
    for load in loads:
        load.start()
    for load, store in zip(loads, stores):
        load.wait()
        store.start()
    for store in stores:
        store.wait()


def shards(ny, embeddings, targets, classes, start_coef):
    rows_here, feats = embeddings.shape
    resp = targets.shape[1]
    all_rows = rows_here * lax.axis_size("row")
    nc = lax.axis_size("col")
    nz = lax.axis_size("row") // ny
    row_tiles = rows_here // LANES
    pieces = feats // ny // LANES
    vmem = pltpu.VMEM
    outs = (
        jax.ShapeDtypeStruct((resp, feats), F32),
        jax.ShapeDtypeStruct((resp, rows_here), F32),
        jax.ShapeDtypeStruct((resp, feats), F32),
    )
    results = pl.pallas_call(
        functools.partial(kernel, ny, nz, nc, resp, float(all_rows)),
        out_shape=outs,
        in_specs=[pl.BlockSpec(memory_space=pltpu.HBM)] * 4,
        out_specs=(pl.BlockSpec(memory_space=pl.ANY),) * 3,
        scratch_shapes=[
            *(vmem(out.shape, F32) for out in outs),
            vmem((rows_here, feats), BF16),
            vmem((resp, rows_here), F32),
            vmem((row_tiles, LANES), jnp.int32),
            vmem((resp, feats), F32),
            vmem((resp, feats), BF16),
            vmem((resp, rows_here), F32),
            vmem((resp, feats), F32),
            vmem((CORES, row_tiles // CORES, LANES), F32),
            vmem((row_tiles, resp, LANES), F32),
            vmem((2 * resp, rows_here), BF16),
            vmem((resp, feats), F32),
            vmem((2, row_tiles, resp, LANES), F32),
            vmem((2, row_tiles // CORES, resp, LANES), F32),
            vmem((2, nc // CORES, row_tiles // CORES, resp, LANES), F32),
            vmem((2, row_tiles, resp, LANES), F32),
            vmem((2, ny, pieces, resp, LANES), F32),
            vmem((2, ny, pieces, resp, LANES), F32),
            vmem((2, pieces, resp, LANES), F32),
            vmem((2, max(nz, ny * pieces), resp, LANES), F32),
            vmem((2, ny, pieces, resp, LANES), F32),
            vmem((nc, 1, LANES), F32),
            vmem((ny, 1, LANES), F32),
            vmem((nz, 1, LANES), F32),
            vmem((nc * ny * pieces, 1, LANES), F32),
            pltpu.SemaphoreType.DMA((3 + CORES,)),
            pltpu.SemaphoreType.DMA((N_SEMS,)),
            pltpu.SemaphoreType.DMA((N_SEMS,)),
            pltpu.SemaphoreType.REGULAR((4,)),
            pltpu.SemaphoreType.DMA((3,)),
        ],
        compiler_params=pltpu.CompilerParams(
            collective_id=0, has_side_effects=True, vmem_limit_bytes=60 * 1024 * 1024),
    )(embeddings, targets.T, classes.reshape(row_tiles, LANES), start_coef.T)
    results = pl.pallas_call(
        write_out,
        out_shape=outs,
        in_specs=[pl.BlockSpec(memory_space=pl.ANY)] * 3,
        out_specs=(pl.BlockSpec(memory_space=pl.ANY),) * 3,
        scratch_shapes=[*(vmem(out.shape, F32) for out in outs), pltpu.SemaphoreType.DMA((2, 3))],
        compiler_params=pltpu.CompilerParams(vmem_limit_bytes=60 * 1024 * 1024),
    )(*results)
    return tuple(out.T for out in results)


def solution(mesh, y_chips=Y_CHIPS):
    return jax.shard_map(
        functools.partial(shards, y_chips),
        mesh=mesh,
        in_specs=(P("row", "col"), P("row", None), P("row"), P("col", None)),
        out_specs=(P("col", None), P("row", None), P("col", None)),
        check_vma=False,
    )
```

```python
import functools

import jax
import jax.numpy as jnp
from jax import lax
from jax.experimental import pallas as pl
from jax.experimental.pallas import tpu as pltpu
from jax.sharding import PartitionSpec as P

MESH = pl.DeviceIdType.MESH
BF16 = jnp.bfloat16
F32 = jnp.float32
huber_delta = 8.0
LANES = 128
Y_CHIPS = 4
CORES = 2

(CORE1, X1, BACK1, Y1, Z1, GAMMA, CORE2, X2, BACK2, SCAL_Y, SCAL_Z, Y2, Z2, SQUARE, G1) = range(15)
G2 = G1 + Y_CHIPS
N_SEMS = G2 + Y_CHIPS


def drain(ref, sem):
    pltpu.make_async_copy(ref, ref, sem).wait()


def kernel(ny, nz, nc, resp, all_rows,
           e_hbm, t_hbm, cls_hbm, c_hbm,
           coef_hbm, resid_hbm, dir_hbm,
           coef_out, resid_out, dir_out,
           e, t, cls, coef, cb, acc, gacc, w, resid, lhs, g,
           part, crecv, xsum, xfull, yrecv, ypart, ysum, zrecv, gath,
           row_x, row_y, row_z, row_sq,
           load_sem, send_sem, recv_sem, near_sem, out_sem):
    rows_here, feats = e.shape
    row_tiles = rows_here // LANES
    half_rows = rows_here // CORES
    half_tiles = row_tiles // CORES
    quarter = feats // ny
    pieces = quarter // LANES
    nx = nc // CORES
    near = nz // 8
    here = lax.axis_index("row")
    col = lax.axis_index("col")
    y, z = lax.div(here, nz), lax.rem(here, nz)
    x, core = lax.div(col, CORES), lax.rem(col, CORES)
    my_piece = lax.rem(z, pieces)
    theirs = 1 - core

    def tile_at(j):
        return pl.ds(pl.multiple_of(j * LANES, LANES), LANES)

    def rows_of(k):
        return pl.ds(pl.multiple_of(k * half_rows, half_rows), half_rows)

    def tiles_of(k):
        return pl.ds(k * half_tiles, half_tiles)

    def far_first(n):
        return [n // 2 + ((k + 1) // 2) * (2 * (k % 2) - 1) for k in range(n - 1)]

    def at_yz(dy, dz):
        return lax.rem(y + dy + ny, ny) * nz + lax.rem(z + dz + nz, nz), col

    def at_col(dc):
        return here, lax.rem(col + dc, nc)

    other_core = (here, col + 1 - 2 * core)
    x_mates = [(here, lax.rem(x + dx, nx) * CORES + core) for dx in far_first(nx)]
    col_mates = [at_col(dc) for dc in far_first(nc)]
    spread = [(dy, dz) for dz in sorted(range(1 - pieces // 2, pieces // 2 + 1), key=lambda d: -abs(d))
              for dy in [*far_first(ny), 0] if (dy, dz) != (0, 0)]

    def send(which, src, dst, peer):
        pltpu.make_async_remote_copy(
            src_ref=src, dst_ref=dst,
            send_sem=send_sem.at[which], recv_sem=recv_sem.at[which],
            device_id=peer, device_id_type=MESH,
        ).start()

    load_c = pltpu.make_async_copy(c_hbm, coef, load_sem.at[0])
    load_t = pltpu.make_async_copy(t_hbm, t, load_sem.at[1])
    load_cls = pltpu.make_async_copy(cls_hbm, cls, load_sem.at[2])
    load_e = [pltpu.make_async_copy(
        e_hbm.at[rows_of(k)], e.at[rows_of(k)], load_sem.at[3 + i]) for i, k in enumerate((theirs, core))]
    load_c.start()
    for load in load_e:
        load.start()
    load_t.start()
    load_cls.start()

    barrier = pltpu.get_barrier_semaphore()
    near_z = [dz for k in range(near) for dz in (near - k, k - near)]
    greeted = [*x_mates, *(at_yz(dy, 0) for dy in far_first(ny)), *(at_yz(0, dz) for dz in near_z), other_core]
    for peer in greeted:
        pl.semaphore_signal(barrier, inc=1, device_id=peer, device_id_type=MESH)

    def tell(k, reach):
        for i, dz in enumerate((reach, -reach)):
            pl.semaphore_signal(near_sem.at[2 * k + i], inc=1, device_id=at_yz(0, dz), device_id_type=MESH)

    def hear(k):
        for i in range(2):
            pl.semaphore_wait(near_sem.at[2 * k + i], 1)

    def meet():
        pl.semaphore_wait(barrier, len(greeted))
        tell(0, near)

    def against_rows(left, rows, lanes):
        return lax.dot_general(
            left, e[rows, lanes], (((1,), (1,)), ((), ())), preferred_element_type=F32)

    def x_reduce(which_core, which_x, which_back, buf, product, before_send, between):
        for i, k in enumerate((theirs, core)):
            both = product(rows_of(k), i)
            for j in range(half_tiles):
                part[buf, k * half_tiles + j] = both[:, j * LANES:(j + 1) * LANES]
            if i == 0:
                before_send()
                send(which_core, part.at[buf, tiles_of(k)], crecv.at[buf], other_core)
        between()
        drain(crecv.at[buf], recv_sem.at[which_core])
        xsum[buf, x] = part[buf, tiles_of(core)] + crecv[buf]
        for mate in x_mates:
            send(which_x, xsum.at[buf, x], xsum.at[buf, x], mate)
        drain(xsum.at[buf, pl.ds(0, nx - 1)], recv_sem.at[which_x])
        total = xsum[buf, 0]
        for k in range(1, nx):
            total = total + xsum[buf, k]
        xfull[buf, tiles_of(core)] = total
        send(which_back, xfull.at[buf, tiles_of(core)], xfull.at[buf, tiles_of(core)], other_core)

    def x_halves(which_back, buf, of_half):
        for i, k in enumerate((core, theirs)):
            if i == 1:
                drain(crecv.at[buf], recv_sem.at[which_back])
            of_half(i, k)
            if i == 0:
                both = jnp.dot(lhs[:, rows_of(k)], e[rows_of(k), :], preferred_element_type=F32)
                gacc[...] = both[:resp] + both[resp:]

    def y_reduce(which, buf):
        for dy in [*far_first(ny), 0]:
            other = lax.rem(y + dy, ny)
            lanes = pl.ds(pl.multiple_of(other * quarter, quarter), quarter)
            both = jnp.dot(lhs[:, rows_of(theirs)], e[rows_of(theirs), lanes], preferred_element_type=F32)
            total = gacc[:, lanes] + both[:resp] + both[resp:]
            into = ypart.at[buf, other] if dy else yrecv.at[buf, y]
            for p in range(pieces):
                into[p] = total[:, p * LANES:(p + 1) * LANES]
            if dy:
                send(which, ypart.at[buf, other], yrecv.at[buf, y], at_yz(dy, 0))

    def z_reduce(which_y, which_z, buf):
        drain(yrecv.at[buf, pl.ds(0, ny - 1)], recv_sem.at[which_y])
        total = yrecv[buf, 0]
        for k in range(1, ny):
            total = total + yrecv[buf, k]
        ysum[buf] = total
        for dz in far_first(nz):
            peer_piece = lax.rem(z + dz, pieces)
            send(which_z, ysum.at[buf, peer_piece], zrecv.at[buf, z], at_yz(0, dz))
        zrecv[buf, z] = ysum[buf, my_piece]

    def spread_out(which_z, which_g, buf, change, first=lambda total: None):
        drain(zrecv.at[buf, pl.ds(0, nz - 1)], recv_sem.at[which_z])
        total = zrecv[buf, 0]
        for k in range(1, nz):
            total = total + zrecv[buf, k]
        total = change(total)
        gath[buf, y, my_piece] = total
        first(total)
        for dy, dz in spread:
            send(which_g + dy, gath.at[buf, y, my_piece], gath.at[buf, y, my_piece], at_yz(dy, dz))
        return total

    def collect(which_g, buf, dy):
        drain(zrecv.at[buf, pl.ds(0, pieces if dy else pieces - 1)], recv_sem.at[which_g + dy])
        return lax.rem(y - dy + ny, ny)

    by_arrival = [0, *reversed(far_first(ny))]

    lane = lax.broadcasted_iota(jnp.int32, (resp, LANES), 1)
    sub = lax.broadcasted_iota(jnp.int32, (resp, LANES), 0)
    diagonal = lane == sub

    def to_row(column):
        return jnp.sum(jnp.where(diagonal, column, 0.0), axis=0, keepdims=True)

    def to_column(row):
        return jnp.sum(jnp.where(diagonal, row, 0.0), axis=1, keepdims=True)

    load_c.wait()
    cb[...] = coef[...].astype(BF16)

    def first_product(rows, i):
        load_e[i].wait()
        return against_rows(cb[...], rows, slice(None))

    x_reduce(CORE1, X1, BACK1, 0, first_product, meet, lambda: None)
    load_t.wait()
    load_cls.wait()
    hear(0)
    tell(1, 2 * near)

    def put_pairs(k, values):
        for j, value in enumerate(values):
            high = value.astype(BF16)
            lhs[0:resp, tile_at(k * half_tiles + j)] = high
            lhs[resp:2 * resp, tile_at(k * half_tiles + j)] = (value - high.astype(F32)).astype(BF16)

    def weigh(i, k):
        rs = [t[:, tile_at(k * half_tiles + j)] - xfull[0, k * half_tiles + j] for j in range(half_tiles)]
        norm = jnp.sqrt(jnp.concatenate([jnp.sum(r * r, axis=0, keepdims=True) for r in rs], axis=0))
        huber = jnp.where(k == 0, cls[0:half_tiles], cls[half_tiles:2 * half_tiles]) == 1
        weight = jnp.where(huber, huber_delta / jnp.maximum(huber_delta, norm), 1.0)
        put_pairs(k, [weight[j:j + 1] * r for j, r in enumerate(rs)])
        w[k] = weight
        for j, r in enumerate(rs):
            resid[k * half_tiles + j] = r

    x_halves(BACK1, 0, weigh)

    y_reduce(Y1, 0)
    hear(1)
    z_reduce(Y1, Z1, 0)
    spread_out(Z1, G1, 0, lambda total: total)
    for k, dy in enumerate(by_arrival):
        behind = collect(G1, 0, dy)
        for p in range(pieces):
            lanes = pl.ds(pl.multiple_of(behind * quarter + p * LANES, LANES), LANES)
            piece = gath[0, behind, p]
            g[:, lanes] = piece
            cb[:, lanes] = piece.astype(BF16)
        lanes = pl.ds(pl.multiple_of(behind * quarter, quarter), quarter)
        if k < ny - 1:
            share = against_rows(cb[:, lanes], slice(None), lanes)
            acc[...] = share if k == 0 else acc[...] + share

    def last_product(rows, k):
        return acc[:, rows] + against_rows(cb[:, lanes], rows, lanes)

    def send_gamma():
        norm2 = jnp.zeros((resp, LANES), F32)
        for p in range(ny * pieces):
            piece = g[:, p * LANES:(p + 1) * LANES]
            norm2 = norm2 + piece * piece
        row_x[col] = to_row(jnp.sum(norm2, axis=1, keepdims=True))
        for mate in col_mates:
            send(GAMMA, row_x.at[col], row_x.at[col], mate)

    x_reduce(CORE2, X2, BACK2, 1, last_product, lambda: None, send_gamma)
    curvs = [jnp.zeros((resp, LANES), F32)] * CORES
    weights = [None] * CORES

    def weigh_image(i, k):
        weight = w[k]
        images = [xfull[1, k * half_tiles + j] for j in range(half_tiles)]
        scaled = [weight[j:j + 1] * image for j, image in enumerate(images)]
        put_pairs(k, scaled)
        for j, image in enumerate(images):
            curvs[i] = curvs[i] + scaled[j] * image
        weights[i] = jnp.sum(weight, axis=0, keepdims=True)

    x_halves(BACK2, 1, weigh_image)
    curv, weight_sum = curvs[0] + curvs[1], weights[0] + weights[1]
    row_y[y] = to_row(jnp.sum(curv, axis=1, keepdims=True)) + jnp.where(
        lane[0:1] == resp, jnp.sum(weight_sum, axis=1, keepdims=True), 0.0)
    for dy in far_first(ny):
        send(SCAL_Y, row_y.at[y], row_y.at[y], at_yz(dy, 0))

    y_reduce(Y2, 1)
    drain(row_y.at[pl.ds(0, ny - 1)], recv_sem.at[SCAL_Y])
    row_z[z] = jnp.sum(row_y[...], axis=0)
    for dz in far_first(nz):
        send(SCAL_Z, row_z.at[z], row_z.at[z], at_yz(0, dz))
    z_reduce(Y2, Z2, 1)

    drain(row_x.at[pl.ds(0, nc - 1)], recv_sem.at[GAMMA])
    drain(row_z.at[pl.ds(0, nz - 1)], recv_sem.at[SCAL_Z])
    sums = jnp.sum(row_z[...], axis=0)
    gamma_raw = to_column(jnp.sum(row_x[...], axis=0))
    curv_raw = to_column(sums)
    mean = jnp.sum(jnp.where(lane[0:1] == resp, sums, 0.0), axis=1, keepdims=True) / all_rows
    gamma = gamma_raw / (mean * mean)
    alpha = gamma / (curv_raw / (mean * mean * mean))
    ratio = alpha / mean
    coef_out[...] = coef[...] + alpha * (g[...] / mean)
    for j in range(row_tiles):
        resid_out[:, j * LANES:(j + 1) * LANES] = resid[j] - alpha * (xfull[1, j] / mean)
    stores = [pltpu.make_async_copy(src, dst, out_sem.at[k]) for k, (src, dst) in enumerate(
        ((coef_out, coef_hbm), (resid_out, resid_hbm), (dir_out, dir_hbm)))]
    stores[0].start()
    stores[1].start()

    def piece_of_next(total):
        return g[:, tile_at(y * pieces + my_piece)] - ratio * total

    slot = col * ny * pieces + y * pieces + my_piece

    def send_square(dc, dy, dz):
        send(SQUARE, row_sq.at[slot], row_sq.at[slot], (at_yz(dy, dz)[0], lax.rem(col + dc, nc)))

    def to_column_block(k, _):
        dc = nc // 2 + lax.div(k + 1, 2) * (2 * lax.rem(k, 2) - 1)
        for dy, dz in [*spread, (0, 0)]:
            send_square(dc, dy, dz)
        return 0

    def send_squares(piece):
        row_sq[slot] = to_row(jnp.sum(piece * piece, axis=1, keepdims=True))
        lax.fori_loop(0, nc - 1, to_column_block, 0)
        for dy, dz in spread:
            send_square(0, dy, dz)

    spread_out(Z2, G2, 1, piece_of_next, send_squares)
    for dy in by_arrival:
        collect(G2, 1, dy)
    for other in range(ny):
        for p in range(pieces):
            lanes = slice(other * quarter + p * LANES, other * quarter + (p + 1) * LANES)
            dir_out[:, lanes] = gath[1, other, p] / mean
            g[:, lanes] = g[:, lanes] / mean
    drain(row_sq.at[pl.ds(0, nc * ny * pieces - 1)], recv_sem.at[SQUARE])
    square = to_column(jnp.sum(row_sq[...], axis=0))
    beta = square / (mean * mean) / gamma
    dir_out[...] = dir_out[...] + beta * g[...]
    stores[2].start()

    for which, ref in (
        *((which, crecv.at[0]) for which in (CORE1, BACK1, CORE2, BACK2)),
        *((which, xsum.at[0, pl.ds(0, nx - 1)]) for which in (X1, X2)),
        *((which, yrecv.at[0, pl.ds(0, ny - 1)]) for which in (Y1, Y2)),
        *((which, zrecv.at[0, pl.ds(0, nz - 1)]) for which in (Z1, Z2)),
        *((base + k, zrecv.at[0, pl.ds(0, pieces if k else pieces - 1)]) for base in (G1, G2) for k in range(ny)),
        (GAMMA, row_x.at[pl.ds(0, nc - 1)]), (SCAL_Y, row_y.at[pl.ds(0, ny - 1)]), (SCAL_Z, row_z.at[pl.ds(0, nz - 1)]),
        (SQUARE, row_sq.at[pl.ds(0, nc * ny * pieces - 1)]),
    ):
        drain(ref, send_sem.at[which])
    for store in stores:
        store.wait()


def write_out(a_in, b_in, c_in, a_out, b_out, c_out, a, b, c, sems):
    moves = ((a_in, a, a_out), (b_in, b, b_out), (c_in, c, c_out))
    loads = [pltpu.make_async_copy(src, held, sems.at[0, k]) for k, (src, held, _) in enumerate(moves)]
    stores = [pltpu.make_async_copy(held, dst, sems.at[1, k]) for k, (_, held, dst) in enumerate(moves)]
    for load in loads:
        load.start()
    for load, store in zip(loads, stores):
        load.wait()
        store.start()
    for store in stores:
        store.wait()


def shards(ny, embeddings, targets, classes, start_coef):
    rows_here, feats = embeddings.shape
    resp = targets.shape[1]
    all_rows = rows_here * lax.axis_size("row")
    nc = lax.axis_size("col")
    nz = lax.axis_size("row") // ny
    row_tiles = rows_here // LANES
    pieces = feats // ny // LANES
    vmem = pltpu.VMEM
    outs = (
        jax.ShapeDtypeStruct((resp, feats), F32),
        jax.ShapeDtypeStruct((resp, rows_here), F32),
        jax.ShapeDtypeStruct((resp, feats), F32),
    )
    results = pl.pallas_call(
        functools.partial(kernel, ny, nz, nc, resp, float(all_rows)),
        out_shape=outs,
        in_specs=[pl.BlockSpec(memory_space=pltpu.HBM)] * 4,
        out_specs=(pl.BlockSpec(memory_space=pl.ANY),) * 3,
        scratch_shapes=[
            *(vmem(out.shape, F32) for out in outs),
            vmem((rows_here, feats), BF16),
            vmem((resp, rows_here), F32),
            vmem((row_tiles, LANES), jnp.int32),
            vmem((resp, feats), F32),
            vmem((resp, feats), BF16),
            vmem((resp, rows_here), F32),
            vmem((resp, feats), F32),
            vmem((CORES, row_tiles // CORES, LANES), F32),
            vmem((row_tiles, resp, LANES), F32),
            vmem((2 * resp, rows_here), BF16),
            vmem((resp, feats), F32),
            vmem((2, row_tiles, resp, LANES), F32),
            vmem((2, row_tiles // CORES, resp, LANES), F32),
            vmem((2, nc // CORES, row_tiles // CORES, resp, LANES), F32),
            vmem((2, row_tiles, resp, LANES), F32),
            vmem((2, ny, pieces, resp, LANES), F32),
            vmem((2, ny, pieces, resp, LANES), F32),
            vmem((2, pieces, resp, LANES), F32),
            vmem((2, max(nz, ny * pieces), resp, LANES), F32),
            vmem((2, ny, pieces, resp, LANES), F32),
            vmem((nc, 1, LANES), F32),
            vmem((ny, 1, LANES), F32),
            vmem((nz, 1, LANES), F32),
            vmem((nc * ny * pieces, 1, LANES), F32),
            pltpu.SemaphoreType.DMA((3 + CORES,)),
            pltpu.SemaphoreType.DMA((N_SEMS,)),
            pltpu.SemaphoreType.DMA((N_SEMS,)),
            pltpu.SemaphoreType.REGULAR((4,)),
            pltpu.SemaphoreType.DMA((3,)),
        ],
        compiler_params=pltpu.CompilerParams(
            collective_id=0, has_side_effects=True, vmem_limit_bytes=60 * 1024 * 1024),
    )(embeddings, targets.T, classes.reshape(row_tiles, LANES), start_coef.T)
    results = pl.pallas_call(
        write_out,
        out_shape=outs,
        in_specs=[pl.BlockSpec(memory_space=pl.ANY)] * 3,
        out_specs=(pl.BlockSpec(memory_space=pl.ANY),) * 3,
        scratch_shapes=[*(vmem(out.shape, F32) for out in outs), pltpu.SemaphoreType.DMA((2, 3))],
        compiler_params=pltpu.CompilerParams(vmem_limit_bytes=60 * 1024 * 1024),
    )(*results)
    return tuple(out.T for out in results)


def solution(mesh, y_chips=Y_CHIPS):
    return jax.shard_map(
        functools.partial(shards, y_chips),
        mesh=mesh,
        in_specs=(P("row", "col"), P("row", None), P("row"), P("col", None)),
        out_specs=(P("col", None), P("row", None), P("col", None)),
        check_vma=False,
    )
```
